32 devices in a mesh: groups: 2 (over y), expert: 16 (over z, x, core).
Axes of the slice: x: 2, y: 2, z: 4, core: 2. Of those that a mesh axis runs over, the one named last changes fastest.
Arguments:
- tokens: bfloat16 [1024, 2048], P(('groups', 'expert')), parts along dimension 0, may hold values from -6 to 6
- grad_out: bfloat16 [1024, 2048], P(('groups', 'expert')), parts along dimension 0, may hold values from -6 to 6
- route_prob: float32 [1024], P(('groups', 'expert')), parts along dimension 0, may hold values from 0.25 to 1
- block_expert: int32 [256], P(('groups', 'expert')), parts along dimension 0, may hold values from 0 to 15, as said below
- block_live: int32 [256], P(('groups', 'expert')), parts along dimension 0, may hold values from 2 to 4, as said below
- expert_weights: bfloat16 [16, 3, 2048, 384], P('expert'), may hold values from -0.1875 to 0.1875
Outputs:
- d_tokens: bfloat16 [1024, 2048], P(('groups', 'expert')), parts along dimension 0
- d_prob: float32 [1024], P(('groups', 'expert')), parts along dimension 0
- weight_grads: bfloat16 [32, 3, 2048, 384], P(('groups', 'expert')), parts along dimension 0
The draws below stay inside these ranges and needn't reach their ends.
There are 2 independent parts, one for each index of `groups`. The reference program is written for one: setup_inputs(seed, part) draws one part's arguments, and reference() takes and returns one part's arrays. A program takes and returns all parts, laid end to end along the dimension named above; an argument that names none is the same for every part. Nothing has to cross between parts.
Inputs may be any that keep to these rules, and one draw needn't show every extreme that they name: `block_expert`: on each device the 8 blocks name, in an order drawn per device, exactly one of the two experts e and e + 8 for every e below 8. Every expert is named by 1 to 15 blocks in all, and one expert by exactly 15. `block_live`: some block has 4 live rows and some has 2.
All inputs are finite; a program needn't handle non-finite values.
Results may differ from the reference program's by a relative error of at most 0.0061.
Values may be sent and summed in bfloat16 or wider, within the bound.
A program may use at most 128 MiB of HBM per device.

```python
import jax
import jax.numpy as jnp
from jax import lax

D = 2048
FF = 384
BLK = 4
EXPERTS = 16
NBLK = 8
ROWS = 512


def draw_block_expert(key, part):
    half_size = EXPERTS // 2
    base = jax.random.fold_in(key, 11)
    key_load, key_force, key_pairs, key_order = jax.random.split(base, 4)
    loads = jax.random.randint(key_load, (half_size,), 1, EXPERTS)
    forced = jax.random.randint(key_force, (), 0, half_size)
    pair_ids = jnp.arange(half_size, dtype=jnp.int32)
    loads = jnp.where(pair_ids == forced, EXPERTS - 1, loads)
    pair_keys = jax.random.split(key_pairs, half_size)
    ranks = jax.vmap(lambda subkey: jnp.argsort(jax.random.permutation(subkey, EXPERTS)))(pair_keys)
    lower = ranks < loads[:, None]
    member = jnp.where(lower, pair_ids[:, None], pair_ids[:, None] + half_size)
    order_keys = jax.random.split(key_order, EXPERTS)
    placing = jax.vmap(lambda subkey: jax.random.permutation(subkey, half_size))(order_keys)
    chosen = jnp.take_along_axis(member.T, placing, axis=1)
    return chosen.reshape(-1).astype(jnp.int32)


def draw_block_live(key, part):
    total_blocks = EXPERTS * NBLK
    base = jax.random.fold_in(key, 23)
    key_rows, key_spot = jax.random.split(base, 2)
    live = jax.random.randint(key_rows, (total_blocks,), BLK // 2, BLK + 1)
    spot = jax.random.randint(key_spot, (), 0, total_blocks)
    positions = jnp.arange(total_blocks, dtype=jnp.int32)
    live = jnp.where(positions == spot, BLK, live)
    live = jnp.where(positions == (spot + 1) % total_blocks, BLK // 2, live)
    return live.astype(jnp.int32)


def levels(key, extent, pieces, low, top_value):
    factor_of = 1.0
    for position, shards_of in pieces:
        heights = jax.random.uniform(jax.random.fold_in(jax.random.fold_in(key, 6), position), (shards_of,), jnp.float32, low / len(pieces), top_value / len(pieces))
        factor_of = factor_of * jnp.repeat(jnp.exp(heights), extent[position] // shards_of).reshape((-1,) + (1,) * (len(extent) - 1 - position))
    return factor_of


def noise(key, dims, scale, reach, shards=(), kind=jnp.bfloat16):
    drawn = scale * jax.random.normal(key, dims, jnp.float32)
    if shards:
        drawn = drawn * levels(key, dims, shards, -0.22, 0.18)
    return jnp.clip(drawn, -reach, reach).astype(kind)


def setup_inputs(seed: int = 0, part: int = 0) -> dict:
    key_of = jax.random.split(jax.random.key(seed), 7)
    part_splits = jax.random.split(jax.random.fold_in(key_of[6], part), 7)
    return {
        "tokens": noise(part_splits[0], (ROWS, D), 1.0, 6.0, ((0, 16),)),
        "grad_out": noise(part_splits[1], (ROWS, D), 1.0, 6.0, ((0, 16),)),
        "route_prob": jnp.clip(0.25 + 0.75 * jax.random.uniform(part_splits[2], (ROWS,), jnp.float32) ** levels(part_splits[2], (ROWS,), ((0, 16),), -0.2, 0.2), 0.25, 1.0),
        "block_expert": draw_block_expert(jax.random.fold_in(jax.random.fold_in(key_of[6], part), 71), part),
        "block_live": draw_block_live(jax.random.fold_in(jax.random.fold_in(key_of[6], part), 71), part),
        "expert_weights": noise(key_of[5], (EXPERTS, 3, D, FF), (D // 2) ** -0.5, 0.1875, ((0, 16),)),
    }


def expert_rows(inputs, cotangent, weights):
    gate_proj = jnp.dot(inputs, weights[0], preferred_element_type=jnp.float32)
    up_proj = jnp.dot(inputs, weights[1], preferred_element_type=jnp.float32)
    sigma = jax.nn.sigmoid(gate_proj)
    active = gate_proj * sigma
    hidden = (active * up_proj).astype(jnp.bfloat16)
    produced = jnp.dot(hidden, weights[2].T, preferred_element_type=jnp.float32).astype(jnp.bfloat16)
    pulled = jnp.dot(cotangent, weights[2], preferred_element_type=jnp.float32)
    d_gate = (pulled * up_proj * sigma * (1.0 + gate_proj * (1.0 - sigma))).astype(jnp.bfloat16)
    d_up = (pulled * active).astype(jnp.bfloat16)
    d_input = (jnp.dot(d_gate, weights[0].T, preferred_element_type=jnp.float32)
               + jnp.dot(d_up, weights[1].T, preferred_element_type=jnp.float32)).astype(jnp.bfloat16)
    return hidden, produced, d_gate, d_up, d_input


def weight_terms(inputs, cotangent, hidden, d_gate, d_up):
    return jnp.stack([
        jnp.dot(inputs.T, d_gate, preferred_element_type=jnp.float32),
        jnp.dot(inputs.T, d_up, preferred_element_type=jnp.float32),
        jnp.dot(cotangent.T, hidden, preferred_element_type=jnp.float32),
    ])


def reference(tokens, grad_out, route_prob, block_expert, block_live, expert_weights):
    all_blocks = EXPERTS * NBLK
    within = jnp.arange(BLK, dtype=jnp.int32)
    live_rows = within[None, :] < block_live[:, None]
    inputs = jnp.where(live_rows[:, :, None], tokens.reshape(all_blocks, BLK, D), 0)
    scaled = route_prob.reshape(all_blocks, BLK)[:, :, None] * grad_out.reshape(all_blocks, BLK, D).astype(jnp.float32)
    cotangent = jnp.where(live_rows[:, :, None], scaled, 0.0).astype(jnp.bfloat16)
    block_ids = jnp.arange(all_blocks, dtype=jnp.int32)
    source = block_ids // NBLK
    far_side = ((source - block_expert) % EXPERTS) >= EXPERTS // 2

    def per_expert(state, expert):
        produced_all, d_input_all = state
        chosen = jnp.argsort((block_expert != expert).astype(jnp.int32) * all_blocks + block_ids)[:EXPERTS].astype(jnp.int32)
        valid = jnp.take(block_expert, chosen) == expert
        rows_in = jnp.where(valid[:, None, None], jnp.take(inputs, chosen, axis=0), 0).reshape(-1, D)
        rows_cot = jnp.where(valid[:, None, None], jnp.take(cotangent, chosen, axis=0), 0).reshape(-1, D)
        weights = lax.dynamic_index_in_dim(expert_weights, expert, 0, keepdims=False)
        hidden, produced, d_gate, d_up, d_input = expert_rows(rows_in, rows_cot, weights)
        far_rows = jnp.repeat(jnp.take(far_side, chosen) & valid, BLK)
        near_in = jnp.where(far_rows[:, None], 0, rows_in)
        near_cot = jnp.where(far_rows[:, None], 0, rows_cot)
        far_in = jnp.where(far_rows[:, None], rows_in, 0)
        far_cot = jnp.where(far_rows[:, None], rows_cot, 0)
        near_terms = weight_terms(near_in, near_cot, hidden, d_gate, d_up)
        far_terms = lax.optimization_barrier(weight_terms(far_in, far_cot, hidden, d_gate, d_up).astype(jnp.bfloat16))
        total = (near_terms + far_terms.astype(jnp.float32)).astype(jnp.bfloat16)
        produced_blocks = jnp.where(valid[:, None, None], produced.reshape(EXPERTS, BLK, D), 0)
        d_input_blocks = jnp.where(valid[:, None, None], d_input.reshape(EXPERTS, BLK, D), 0)
        produced_all = produced_all.at[chosen].add(produced_blocks)
        d_input_all = d_input_all.at[chosen].add(d_input_blocks)
        return (produced_all, d_input_all), total

    empty = jnp.zeros((all_blocks, BLK, D), jnp.bfloat16)
    (produced_all, d_input_all), weight_grads = lax.scan(per_expert, (empty, empty), jnp.arange(EXPERTS, dtype=jnp.int32))
    d_tokens = d_input_all.reshape(ROWS, D)
    d_prob = jnp.sum(grad_out.astype(jnp.float32) * produced_all.reshape(ROWS, D).astype(jnp.float32), axis=1)
    return d_tokens, d_prob, weight_grads
```

```python
import functools

import jax
import jax.numpy as jnp
from jax import lax
from jax.experimental import pallas as pl
from jax.experimental.pallas import tpu as pltpu
from jax.sharding import PartitionSpec as P

MESH = pl.DeviceIdType.MESH
SLOT = 16
F32 = jnp.float32
BF16 = jnp.bfloat16


def dot(a, b):
    return jnp.dot(a, b, preferred_element_type=F32)


def dot_nt(a, b):
    return lax.dot_general(a, b, (((1,), (1,)), ((), ())), preferred_element_type=F32)


def dot_tn(a, b):
    return lax.dot_general(a, b, (((0,), (0,)), ((), ())), preferred_element_type=F32)


def kernel(
    n, blk, group,
    tok_hbm, go_hbm, prob_hbm, be_hbm, live_hbm, w_ref,
    dtok_ref, dprob_ref, wg_ref,
    tok_ref, go_ref, prob_ref, be_ref, live_ref, wcat, wdown, send_x, send_c, got_x, got_c, send_d, got_d, send_t, got_t,
    rows_x, rows_c, d_cat, hid,
    in_sem, w_sem, sx_sem, rx_sem, sc_sem, rc_sem, sd_sem, rd_sem, st_sem, rt_sem,
):
    me = lax.axis_index("expert")
    rows, width = tok_ref.shape
    ff = wdown.shape[1]
    nblk = rows // blk
    parts = SLOT // blk
    pw = width // parts
    cols = parts * rows
    span = group * SLOT
    grow = group * blk
    lanes = prob_ref.shape[1]

    half = n // 2
    side = me // half * half
    place = me % half

    def others(body):
        def across(k, carry):
            body(half - side + (place + k) % half)
            return carry

        def beside(k, carry):
            body(side + (place + k) % half)
            return carry

        lax.fori_loop(0, half, across, 0)
        lax.fori_loop(1, half, beside, 0)

    def slot(ref, i):
        return ref.at[pl.ds(pl.multiple_of(i * SLOT, SLOT), SLOT), :]

    def remote(src, dst, ssem, rsem, to):
        return pltpu.make_async_remote_copy(
            src_ref=src, dst_ref=dst, send_sem=ssem, recv_sem=rsem,
            device_id={"expert": to}, device_id_type=MESH,
        )

    def send(src, dst, ssem, rsem):
        others(lambda to: remote(slot(src, to), slot(dst, me), ssem, rsem, to).start())

    def every_slot(src, dst, ssem, rsem):
        part = pl.ds(0, (n - 1) * SLOT)
        return remote(src.at[part, :], dst.at[part, :], ssem, rsem, (me + 1) % n)

    barrier = pltpu.get_barrier_semaphore()
    others(
        lambda to: pl.semaphore_signal(
            barrier, inc=1, device_id={"expert": to}, device_id_type=MESH
        )
    )
    inputs = [
        pltpu.make_async_copy(src, dst, in_sem.at[j])
        for j, (src, dst) in enumerate(
            (
                (be_hbm, be_ref), (live_hbm, live_ref), (prob_hbm, prob_ref),
                (tok_hbm, tok_ref), (go_hbm, go_ref),
            )
        )
    ]
    for load in inputs:
        load.start()
    loads = [
        pltpu.make_async_copy(w_ref.at[0, 0], wcat.at[:, pl.ds(0, ff)], w_sem.at[0]),
        pltpu.make_async_copy(w_ref.at[0, 1], wcat.at[:, pl.ds(ff, ff)], w_sem.at[1]),
        pltpu.make_async_copy(w_ref.at[0, 2], wdown, w_sem.at[2]),
    ]
    for load in loads:
        load.start()
    for load in inputs:
        load.wait()

    def keys(shape, axis):
        k = lax.broadcasted_iota(jnp.int32, shape, axis)
        part, row = k // rows, k % rows
        block, within = row // blk, row % blk
        owner = jnp.zeros(shape, jnp.int32)
        live = jnp.zeros(shape, jnp.int32)
        for b in range(nblk):
            owner = jnp.where(block == b, be_ref[b], owner)
            live = jnp.where(block == b, live_ref[b], live)
        return jnp.where(within < live, owner * SLOT + part * blk + within, -1)

    def stacked(value):
        return jnp.concatenate([value[:, p * pw:(p + 1) * pw] for p in range(parts)], axis=0)

    def one_hot(mask):
        return jnp.where(mask, 1.0, 0.0).astype(BF16)

    probs = []
    for g in range(rows // lanes):
        square = (lanes, lanes)
        diagonal = lax.broadcasted_iota(jnp.int32, square, 0) == lax.broadcasted_iota(
            jnp.int32, square, 1
        )
        line = jnp.broadcast_to(prob_ref[g:g + 1, :], square)
        probs.append(jnp.sum(jnp.where(diagonal, line, 0.0), axis=1, keepdims=True))
    prob = jnp.concatenate(probs, axis=0) if len(probs) > 1 else probs[0]
    tok4 = stacked(tok_ref[...])
    cot4 = stacked((prob * go_ref[...].astype(F32)).astype(BF16))
    key_row = keys((1, cols), 1)

    def pack(c, carry):
        at = pl.multiple_of(c * span, span)
        ids = lax.broadcasted_iota(jnp.int32, (span, cols), 0) + c * span
        pick = one_hot(ids == key_row)
        send_x[pl.ds(at, span), :] = dot(pick, tok4).astype(BF16)
        send_c[pl.ds(at, span), :] = dot(pick, cot4).astype(BF16)
        return carry

    lax.fori_loop(0, n // group, pack, 0)
    pl.semaphore_wait(barrier, n - 1)
    send(send_x, got_x, sx_sem, rx_sem)
    send(send_c, got_c, sc_sem, rc_sem)
    slot(got_x, me)[...] = slot(send_x, me)[...]
    slot(got_c, me)[...] = slot(send_c, me)[...]

    i = lax.broadcasted_iota(jnp.int32, (span, span), 0)
    k = lax.broadcasted_iota(jnp.int32, (span, span), 1)
    unslot = one_hot(k == ((i % grow) // blk) * SLOT + (i // grow) * blk + i % blk)
    toslot = one_hot(i == ((k % grow) // blk) * SLOT + (k // grow) * blk + k % blk)

    def unpack(got, into):
        def step(c, carry):
            at = pl.multiple_of(c * span, span)
            out = pl.multiple_of(c * grow, grow)
            value = dot(unslot, got[pl.ds(at, span), :]).astype(BF16)
            for p in range(parts):
                into[pl.ds(out, grow), p * pw:(p + 1) * pw] = value[p * grow:(p + 1) * grow, :]
            return carry

        lax.fori_loop(0, n // group, step, 0)

    every_slot(send_x, got_x, sx_sem, rx_sem).wait_recv()
    unpack(got_x, rows_x)
    for load in loads:
        load.wait()

    def forward(c, carry):
        out = pl.multiple_of(c * grow, grow)
        d_cat[pl.ds(out, grow), :] = dot(rows_x[pl.ds(out, grow), :], wcat[...])
        return carry

    lax.fori_loop(0, n // group, forward, 0)
    every_slot(send_c, got_c, sc_sem, rc_sem).wait_recv()
    unpack(got_c, rows_c)

    def backward(c, carry):
        out = pl.multiple_of(c * grow, grow)
        here = pl.ds(out, grow)
        gate, up = d_cat[here, :ff], d_cat[here, ff:]
        pulled = dot(rows_c[here, :], wdown[...])
        sigma = jax.nn.sigmoid(gate)
        active = gate * sigma
        hidden = (active * up).astype(BF16)
        hid[here, :] = hidden
        share = jnp.sum(hidden.astype(F32) * pulled, axis=1, keepdims=True)
        share = jnp.broadcast_to(share, (grow, send_t.shape[2]))
        for j in range(group):
            send_t[c * group + j] = share[j * blk:(j + 1) * blk, :]
        d_cat[here, :ff] = pulled * up * sigma * (1.0 + gate * (1.0 - sigma))
        d_cat[here, ff:] = pulled * active
        return carry

    lax.fori_loop(0, n // group, backward, 0)

    others(lambda to: remote(send_t.at[to], got_t.at[me], st_sem, rt_sem, to).start())
    every_t = remote(
        send_t.at[pl.ds(0, n - 1)], got_t.at[pl.ds(0, n - 1)], st_sem, rt_sem, (me + 1) % n
    )
    got_t[me] = send_t[me]

    def rows_back(c, carry):
        at = pl.multiple_of(c * span, span)
        here = pl.ds(pl.multiple_of(c * grow, grow), grow)
        d_in = dot_nt(d_cat[here, :].astype(BF16), wcat[...]).astype(BF16)
        send_d[pl.ds(at, span), :] = dot(toslot, stacked(d_in)).astype(BF16)
        return carry

    lax.fori_loop(0, n // group, rows_back, 0)
    send(send_d, got_d, sd_sem, rd_sem)
    slot(got_d, me)[...] = slot(send_d, me)[...]

    d_all = d_cat[...].astype(BF16)
    for p in range(parts):
        here = pl.ds(p * pw, pw)
        grads = dot_tn(rows_x[:, here], d_all).astype(BF16)
        wg_ref[0, 0, here, :] = grads[:, :ff]
        wg_ref[0, 1, here, :] = grads[:, ff:]
        wg_ref[0, 2, here, :] = dot_tn(rows_c[:, here], hid[...]).astype(BF16)

    every_t.wait_recv()
    lane = lax.broadcasted_iota(jnp.int32, (blk, got_t.shape[2]), 1)
    row = lax.broadcasted_iota(jnp.int32, (blk, got_t.shape[2]), 0)
    per = lanes // blk
    for g in range(rows // lanes):
        line = jnp.zeros((blk, got_t.shape[2]), F32)
        for j in range(per):
            line = jnp.where(lane == j * blk + row, got_t[be_ref[g * per + j]], line)
        total = jnp.sum(line, axis=0, keepdims=True)[:, :lanes]
        dprob_ref[g:g + 1, :] = total / prob_ref[g:g + 1, :]

    key_column = keys((cols, 1), 0)
    every_slot(send_d, got_d, sd_sem, rd_sem).wait_recv()

    def home(c, total):
        at = pl.multiple_of(c * span, span)
        ids = lax.broadcasted_iota(jnp.int32, (cols, span), 1) + c * span
        return total + dot(one_hot(ids == key_column), got_d[pl.ds(at, span), :])

    total = home(0, jnp.zeros((cols, pw), F32))
    if n // group > 1:
        total = lax.fori_loop(1, n // group, home, total)
    for p in range(parts):
        dtok_ref[:, p * pw:(p + 1) * pw] = total[p * rows:(p + 1) * rows, :].astype(BF16)

    every_slot(send_x, got_x, sx_sem, rx_sem).wait_send()
    every_slot(send_c, got_c, sc_sem, rc_sem).wait_send()
    every_slot(send_d, got_d, sd_sem, rd_sem).wait_send()
    every_t.wait_send()


def store_kernel(*refs):
    count = len(refs) // 2
    sems = refs[-1]
    stores = [
        pltpu.make_async_copy(src, dst, sems.at[j])
        for j, (src, dst) in enumerate(zip(refs[:count], refs[count:2 * count]))
    ]
    for store in stores:
        store.start()
    for store in stores:
        store.wait()


def shards(n, tokens, grad_out, route_prob, block_expert, block_live, expert_weights):
    rows, width = tokens.shape
    blk = rows // block_expert.shape[0]
    ff = expert_weights.shape[3]
    parts = SLOT // blk
    pw = width // parts
    group = min(n, 16)
    lanes = min(rows, 128)
    slots = (n * SLOT, pw)
    every = n * blk
    vmem = pl.BlockSpec(memory_space=pltpu.VMEM)
    any_ = pl.BlockSpec(memory_space=pl.ANY)
    dma = pltpu.SemaphoreType.DMA
    shapes = (
        ((rows, width), BF16),
        ((rows // lanes, lanes), F32),
        ((1, 3, width, ff), BF16),
    )
    results = pl.pallas_call(
        functools.partial(kernel, n, blk, group),
        out_shape=tuple(pltpu.VMEM(*shape) for shape in shapes),
        in_specs=[any_] * 6,
        out_specs=(vmem,) * 3,
        scratch_shapes=[
            pltpu.VMEM((rows, width), BF16),
            pltpu.VMEM((rows, width), BF16),
            pltpu.VMEM((rows // lanes, lanes), F32),
            pltpu.SMEM(block_expert.shape, jnp.int32),
            pltpu.SMEM(block_live.shape, jnp.int32),
            pltpu.VMEM((width, 2 * ff), BF16),
            pltpu.VMEM((width, ff), BF16),
            *[pltpu.VMEM(slots, BF16) for _ in range(6)],
            *[pltpu.VMEM((n, blk, 128), F32) for _ in range(2)],
            pltpu.VMEM((every, width), BF16),
            pltpu.VMEM((every, width), BF16),
            pltpu.VMEM((every, 2 * ff), F32),
            pltpu.VMEM((every, ff), BF16),
            dma((5,)),
            dma((3,)),
            *[dma for _ in range(8)],
        ],
        compiler_params=pltpu.CompilerParams(
            collective_id=0, has_side_effects=True, vmem_limit_bytes=52 * 1024 * 1024
        ),
        cost_estimate=pl.CostEstimate(
            flops=2 * every * width * ff * 8,
            bytes_accessed=2 * 3 * width * ff * 2,
            transcendentals=every * ff,
        ),
    )(
        *[
            pltpu.with_memory_space_constraint(value, pltpu.HBM)
            for value in (
                tokens, grad_out, route_prob.reshape(rows // lanes, lanes),
                block_expert, block_live, expert_weights,
            )
        ]
    )
    d_tokens, d_prob, weight_grads = pl.pallas_call(
        store_kernel,
        out_shape=tuple(jax.ShapeDtypeStruct(*shape) for shape in shapes),
        in_specs=[vmem] * 3,
        out_specs=(any_,) * 3,
        scratch_shapes=[dma((3,))],
        compiler_params=pltpu.CompilerParams(vmem_limit_bytes=1024 * 1024),
    )(*results)
    return (d_tokens, d_prob.reshape(rows), weight_grads)


def solution(mesh):
    placed = (
        P(("groups", "expert"), None),
        P(("groups", "expert"), None),
        P(("groups", "expert")),
        P(("groups", "expert")),
        P(("groups", "expert")),
        P("expert", None, None, None),
    )
    return jax.shard_map(
        functools.partial(shards, mesh.shape["expert"]),
        mesh=mesh,
        in_specs=placed,
        out_specs=(
            P(("groups", "expert"), None),
            P(("groups", "expert")),
            P(("groups", "expert"), None, None, None),
        ),
        check_vma=False,
    )
```

```python
import functools

import jax
import jax.numpy as jnp
from jax import lax
from jax.experimental import pallas as pl
from jax.experimental.pallas import tpu as pltpu
from jax.sharding import PartitionSpec as P

MESH = pl.DeviceIdType.MESH
SLOT = 16
F32 = jnp.float32
BF16 = jnp.bfloat16


def dot(a, b):
    return jnp.dot(a, b, preferred_element_type=F32)


def dot_nt(a, b):
    return lax.dot_general(a, b, (((1,), (1,)), ((), ())), preferred_element_type=F32)


def dot_tn(a, b):
    return lax.dot_general(a, b, (((0,), (0,)), ((), ())), preferred_element_type=F32)


def kernel(
    n, blk, group,
    tok_hbm, go_hbm, prob_hbm, be_hbm, live_hbm, w_ref,
    got_d, back_ref, dprob_ref, wg_ref,
    tok_ref, go_ref, prob_ref, be_ref, live_ref, wcat, wdown,
    send_x, send_c, got_x, got_c, send_d, send_t, got_t, rows_x, rows_c, d_cat, hid,
    in_sem, w_sem, sx_sem, rx_sem, sc_sem, rc_sem, sd_sem, rd_sem, st_sem, rt_sem,
):
    me = lax.axis_index("expert")
    rows, width = tok_ref.shape
    ff = wdown.shape[1]
    nblk = rows // blk
    parts = SLOT // blk
    pw = width // parts
    cols = parts * rows
    lanes = prob_ref.shape[1]
    half = n // 2
    mid = half + half // 2
    side = me // half * half
    place = me % half

    def ahead(k):
        base = jnp.where(k < half, side, half - side)
        return base + (place + k) % half

    def behind(k):
        base = jnp.where(k < half, side, half - side)
        return base + (place - k + n) % half

    def slots(first, last, body):
        def step(k, carry):
            body(k)
            return carry

        lax.fori_loop(first, last, step, 0)

    def part_of(ref, first, count):
        if len(ref.shape) == 3:
            return ref.at[pl.ds(first, count)]
        start = first * SLOT
        if not isinstance(first, int):
            start = pl.multiple_of(start, SLOT)
        return ref.at[pl.ds(start, count * SLOT), :]

    def remote(src, dst, ssem, rsem, to, first, count):
        return pltpu.make_async_remote_copy(
            src_ref=part_of(src, first, count), dst_ref=part_of(dst, first, count),
            send_sem=ssem, recv_sem=rsem,
            device_id={"expert": to}, device_id_type=MESH,
        )

    def send(first, last, src, dst, ssem, rsem, where):
        slots(first, last, lambda k: remote(src, dst, ssem, rsem, where(k), k, 1).start())

    def whole(first, last, src, dst, ssem, rsem):
        return remote(src, dst, ssem, rsem, ahead(1), first, last - first)

    barrier = pltpu.get_barrier_semaphore()
    slots(
        1, n,
        lambda k: pl.semaphore_signal(
            barrier, inc=1, device_id={"expert": ahead(k)}, device_id_type=MESH
        ),
    )
    inputs = [
        pltpu.make_async_copy(src, dst, in_sem.at[j])
        for j, (src, dst) in enumerate(
            (
                (be_hbm, be_ref), (live_hbm, live_ref), (tok_hbm, tok_ref),
                (prob_hbm, prob_ref), (go_hbm, go_ref),
            )
        )
    ]
    for load in inputs:
        load.start()
    loads = [
        pltpu.make_async_copy(w_ref.at[0, 0], wcat.at[:, pl.ds(0, ff)], w_sem.at[0]),
        pltpu.make_async_copy(w_ref.at[0, 1], wcat.at[:, pl.ds(ff, ff)], w_sem.at[1]),
        pltpu.make_async_copy(w_ref.at[0, 2], wdown, w_sem.at[2]),
    ]
    for load in loads:
        load.start()

    def slot_of(expert):
        return (expert % half - place + half) % half + jnp.where(
            expert // half * half == side, 0, half
        )

    def keys(shape, axis):
        k = lax.broadcasted_iota(jnp.int32, shape, axis)
        part, row = k // rows, k % rows
        block, within = row // blk, row % blk
        owner = jnp.zeros(shape, jnp.int32)
        live = jnp.zeros(shape, jnp.int32)
        for b in range(nblk):
            owner = jnp.where(block == b, slot_of(be_ref[b]), owner)
            live = jnp.where(block == b, live_ref[b], live)
        return jnp.where(within < live, owner * SLOT + part * blk + within, -1)

    def stacked(value):
        return jnp.concatenate([value[:, p * pw:(p + 1) * pw] for p in range(parts)], axis=0)

    def one_hot(mask):
        return jnp.where(mask, 1.0, 0.0).astype(BF16)

    bulk = min(n, 16) * SLOT

    def pack(value, into):
        def step(c, carry):
            at = pl.multiple_of(c * bulk, bulk)
            ids = lax.broadcasted_iota(jnp.int32, (bulk, cols), 0) + c * bulk
            into[pl.ds(at, bulk), :] = dot(one_hot(ids == key_row), value).astype(BF16)
            return carry

        lax.fori_loop(0, n * SLOT // bulk, step, 0)

    for load in inputs[:3]:
        load.wait()
    key_row = keys((1, cols), 1)
    pack(stacked(tok_ref[...]), send_x)
    pl.semaphore_wait(barrier, n - 1)
    send(half, mid, send_x, got_x, sx_sem.at[0], rx_sem.at[0], ahead)
    send(1, half, send_x, got_x, sx_sem.at[0], rx_sem.at[0], ahead)

    for load in inputs[3:]:
        load.wait()
    probs = []
    for g in range(rows // lanes):
        square = (lanes, lanes)
        diagonal = lax.broadcasted_iota(jnp.int32, square, 0) == lax.broadcasted_iota(
            jnp.int32, square, 1
        )
        line = jnp.broadcast_to(prob_ref[g:g + 1, :], square)
        probs.append(jnp.sum(jnp.where(diagonal, line, 0.0), axis=1, keepdims=True))
    prob = jnp.concatenate(probs, axis=0) if len(probs) > 1 else probs[0]
    pack(stacked((prob * go_ref[...].astype(F32)).astype(BF16)), send_c)
    send(half, mid, send_c, got_c, sc_sem.at[0], rc_sem.at[0], ahead)
    send(1, half, send_c, got_c, sc_sem.at[0], rc_sem.at[0], ahead)
    send(mid, n, send_x, got_x, sx_sem.at[1], rx_sem.at[1], ahead)
    send(mid, n, send_c, got_c, sc_sem.at[1], rc_sem.at[1], ahead)
    got_x[:SLOT, :] = send_x[:SLOT, :]
    got_c[:SLOT, :] = send_c[:SLOT, :]

    key_column = keys((cols, 1), 0)

    def pick_back(c, carry):
        at = pl.multiple_of(c * bulk, bulk)
        ids = lax.broadcasted_iota(jnp.int32, (cols, bulk), 1) + c * bulk
        back_ref[:, pl.ds(at, bulk)] = one_hot(ids == key_column)
        return carry

    lax.fori_loop(0, n * SLOT // bulk, pick_back, 0)

    class Chunk:
        def __init__(self, first, last, count):
            self.first, self.last, self.count = first, last, count
            self.span, self.grow = count * SLOT, count * blk
            i = lax.broadcasted_iota(jnp.int32, (self.span, self.span), 0)
            k = lax.broadcasted_iota(jnp.int32, (self.span, self.span), 1)
            grow = self.grow
            self.unslot = one_hot(k == (i % grow) // blk * SLOT + i // grow * blk + i % blk)
            self.toslot = one_hot(i == (k % grow) // blk * SLOT + k // grow * blk + k % blk)

        def each(self, body):
            def step(c, carry):
                first = self.first + c * self.count
                body(
                    first,
                    pl.ds(pl.multiple_of(first * SLOT, SLOT), self.span),
                    pl.ds(pl.multiple_of(first * blk, SLOT), self.grow),
                )
                return carry

            lax.fori_loop(0, (self.last - self.first) // self.count, step, 0)

        def unpack(self, got, into):
            def body(first, slot_rows, here):
                value = dot(self.unslot, got[slot_rows, :]).astype(BF16)
                for p in range(parts):
                    into[here, p * pw:(p + 1) * pw] = value[p * self.grow:(p + 1) * self.grow, :]

            self.each(body)

        def forward(self):
            def body(first, slot_rows, here):
                d_cat[here, :] = dot(rows_x[here, :], wcat[...])

            self.each(body)

        def backward(self):
            def body(first, slot_rows, here):
                gate, up = d_cat[here, :ff], d_cat[here, ff:]
                pulled = dot(rows_c[here, :], wdown[...])
                sigma = jax.nn.sigmoid(gate)
                active = gate * sigma
                hidden = (active * up).astype(BF16)
                hid[here, :] = hidden
                share = jnp.sum(hidden.astype(F32) * pulled, axis=1, keepdims=True)
                share = jnp.broadcast_to(share, (self.grow, send_t.shape[2]))
                for j in range(self.count):
                    send_t[first + j] = share[j * blk:(j + 1) * blk, :]
                d_cat[here, :ff] = pulled * up * sigma * (1.0 + gate * (1.0 - sigma))
                d_cat[here, ff:] = pulled * active
                d_in = dot_nt(d_cat[here, :].astype(BF16), wcat[...]).astype(BF16)
                send_d[slot_rows, :] = dot(self.toslot, stacked(d_in)).astype(BF16)

            self.each(body)

    early, late = Chunk(0, mid, 3 * group), Chunk(mid, n, group)
    whole(1, mid, send_x, got_x, sx_sem.at[0], rx_sem.at[0]).wait_recv()
    early.unpack(got_x, rows_x)
    for load in loads:
        load.wait()
    early.forward()
    whole(1, mid, send_c, got_c, sc_sem.at[0], rc_sem.at[0]).wait_recv()
    early.unpack(got_c, rows_c)
    early.backward()
    send(1, half, send_d, got_d, sd_sem, rd_sem, behind)
    got_d[:SLOT, :] = send_d[:SLOT, :]
    whole(mid, n, send_x, got_x, sx_sem.at[1], rx_sem.at[1]).wait_recv()
    late.unpack(got_x, rows_x)
    late.forward()
    whole(mid, n, send_c, got_c, sc_sem.at[1], rc_sem.at[1]).wait_recv()
    send(half, mid, send_d, got_d, sd_sem, rd_sem, behind)
    late.unpack(got_c, rows_c)
    late.backward()
    send(mid, n, send_d, got_d, sd_sem, rd_sem, behind)
    send(1, n, send_t, got_t, st_sem, rt_sem, behind)
    got_t[0] = send_t[0]

    d_all = d_cat[...].astype(BF16)
    for p in range(parts):
        here = pl.ds(p * pw, pw)
        grads = dot_tn(rows_x[:, here], d_all).astype(BF16)
        wg_ref[0, 0, here, :] = grads[:, :ff]
        wg_ref[0, 1, here, :] = grads[:, ff:]
        wg_ref[0, 2, here, :] = dot_tn(rows_c[:, here], hid[...]).astype(BF16)

    every_t = whole(1, n, send_t, got_t, st_sem, rt_sem)
    every_t.wait_recv()
    lane = lax.broadcasted_iota(jnp.int32, (blk, got_t.shape[2]), 1)
    row = lax.broadcasted_iota(jnp.int32, (blk, got_t.shape[2]), 0)
    per = lanes // blk
    for g in range(rows // lanes):
        line = jnp.zeros((blk, got_t.shape[2]), F32)
        for j in range(per):
            line = jnp.where(lane == j * blk + row, got_t[slot_of(be_ref[g * per + j])], line)
        total = jnp.sum(line, axis=0, keepdims=True)[:, :lanes]
        dprob_ref[g:g + 1, :] = total / prob_ref[g:g + 1, :]

    for j, (first, last) in enumerate(((1, mid), (mid, n))):
        whole(first, last, send_x, got_x, sx_sem.at[j], rx_sem.at[j]).wait_send()
        whole(first, last, send_c, got_c, sc_sem.at[j], rc_sem.at[j]).wait_send()
    every_t.wait_send()
    every_d = whole(1, n, send_d, got_d, sd_sem, rd_sem)
    every_d.wait_send()
    every_d.wait_recv()


def store_kernel(got_d, back, d_prob, wg, dtok_hbm, dprob_hbm, wg_hbm, d_tokens, sem):
    stores = [
        pltpu.make_async_copy(wg, wg_hbm, sem.at[0]),
        pltpu.make_async_copy(d_prob, dprob_hbm, sem.at[1]),
        pltpu.make_async_copy(d_tokens, dtok_hbm, sem.at[2]),
    ]
    stores[0].start()
    stores[1].start()
    rows = d_tokens.shape[0]
    pw = got_d.shape[1]
    parts = d_tokens.shape[1] // pw
    for p in range(parts):
        picked = dot(back[p * rows:(p + 1) * rows, :], got_d[...])
        d_tokens[:, p * pw:(p + 1) * pw] = picked.astype(BF16)
    stores[2].start()
    for store in stores:
        store.wait()


def shards(n, tokens, grad_out, route_prob, block_expert, block_live, expert_weights):
    rows, width = tokens.shape
    blk = rows // block_expert.shape[0]
    ff = expert_weights.shape[3]
    parts = SLOT // blk
    pw = width // parts
    group = min(n // 4, 4)
    lanes = min(rows, 128)
    slots = (n * SLOT, pw)
    every = n * blk
    vmem = pl.BlockSpec(memory_space=pltpu.VMEM)
    any_ = pl.BlockSpec(memory_space=pl.ANY)
    dma = pltpu.SemaphoreType.DMA
    shapes = (
        ((rows, width), BF16),
        ((rows // lanes, lanes), F32),
        ((1, 3, width, ff), BF16),
    )
    results = pl.pallas_call(
        functools.partial(kernel, n, blk, group),
        out_shape=(
            pltpu.VMEM(slots, BF16),
            pltpu.VMEM((parts * rows, n * SLOT), BF16),
            *[pltpu.VMEM(*shape) for shape in shapes[1:]],
        ),
        in_specs=[any_] * 6,
        out_specs=(vmem,) * 4,
        scratch_shapes=[
            pltpu.VMEM((rows, width), BF16),
            pltpu.VMEM((rows, width), BF16),
            pltpu.VMEM((rows // lanes, lanes), F32),
            pltpu.SMEM(block_expert.shape, jnp.int32),
            pltpu.SMEM(block_live.shape, jnp.int32),
            pltpu.VMEM((width, 2 * ff), BF16),
            pltpu.VMEM((width, ff), BF16),
            *[pltpu.VMEM(slots, BF16) for _ in range(5)],
            *[pltpu.VMEM((n, blk, 128), F32) for _ in range(2)],
            pltpu.VMEM((every, width), BF16),
            pltpu.VMEM((every, width), BF16),
            pltpu.VMEM((every, 2 * ff), F32),
            pltpu.VMEM((every, ff), BF16),
            dma((5,)),
            dma((3,)),
            *[dma((2,)) for _ in range(4)],
            *[dma for _ in range(4)],
        ],
        compiler_params=pltpu.CompilerParams(
            collective_id=0, has_side_effects=True, vmem_limit_bytes=40 * 1024 * 1024
        ),
        cost_estimate=pl.CostEstimate(
            flops=2 * every * width * ff * 8,
            bytes_accessed=2 * 3 * width * ff * 2,
            transcendentals=every * ff,
        ),
    )(
        *[
            pltpu.with_memory_space_constraint(value, pltpu.HBM)
            for value in (
                tokens, grad_out, route_prob.reshape(rows // lanes, lanes),
                block_expert, block_live, expert_weights,
            )
        ]
    )
    d_tokens, d_prob, weight_grads = pl.pallas_call(
        store_kernel,
        out_shape=tuple(jax.ShapeDtypeStruct(*shape) for shape in shapes),
        in_specs=[vmem] * 4,
        out_specs=(any_,) * 3,
        scratch_shapes=[pltpu.VMEM((rows, width), BF16), dma((3,))],
        compiler_params=pltpu.CompilerParams(vmem_limit_bytes=8 * 1024 * 1024),
    )(*results)
    return (d_tokens, d_prob.reshape(rows), weight_grads)


def solution(mesh):
    placed = (
        P(("groups", "expert"), None),
        P(("groups", "expert"), None),
        P(("groups", "expert")),
        P(("groups", "expert")),
        P(("groups", "expert")),
        P("expert", None, None, None),
    )
    return jax.shard_map(
        functools.partial(shards, mesh.shape["expert"]),
        mesh=mesh,
        in_specs=placed,
        out_specs=(
            P(("groups", "expert"), None),
            P(("groups", "expert")),
            P(("groups", "expert"), None, None, None),
        ),
        check_vma=False,
    )
```

```python
import functools

import jax
import jax.numpy as jnp
from jax import lax
from jax.experimental import pallas as pl
from jax.experimental.pallas import tpu as pltpu
from jax.sharding import PartitionSpec as P

MESH = pl.DeviceIdType.MESH
SLOT = 16
F32 = jnp.float32
BF16 = jnp.bfloat16


def dot(a, b):
    return jnp.dot(a, b, preferred_element_type=F32)


def dot_tn(a, b):
    return lax.dot_general(a, b, (((0,), (0,)), ((), ())), preferred_element_type=F32)


def kernel(
    n, blk, group,
    tok_hbm, go_hbm, prob_hbm, be_hbm, live_hbm, w_ref,
    got_d, back_ref, dprob_ref, wg_ref,
    tok_ref, go_ref, prob_ref, be_ref, live_ref, wcat, wback, wdown,
    send_x, send_c, got_x, got_c, send_d, send_t, got_t, rows_x, rows_c, d_cat, hid,
    in_sem, w_sem, sx_sem, rx_sem, sc_sem, rc_sem, sd_sem, rd_sem, st_sem, rt_sem,
):
    me = lax.axis_index("expert")
    rows, width = tok_ref.shape
    ff = wdown.shape[1]
    nblk = rows // blk
    parts = SLOT // blk
    pw = width // parts
    cols = parts * rows
    lanes = prob_ref.shape[1]
    half = n // 2
    mid = half + half // 2
    side = me // half * half
    place = me % half

    def ahead(k):
        base = jnp.where(k < half, side, half - side)
        return base + (place + k) % half

    def behind(k):
        base = jnp.where(k < half, side, half - side)
        return base + (place - k + n) % half

    def slots(first, last, body):
        def step(k, carry):
            body(k)
            return carry

        lax.fori_loop(first, last, step, 0)

    def part_of(ref, first, count):
        if len(ref.shape) == 3:
            return ref.at[pl.ds(first, count)]
        start = first * SLOT
        if not isinstance(first, int):
            start = pl.multiple_of(start, SLOT)
        return ref.at[pl.ds(start, count * SLOT), :]

    def remote(src, dst, ssem, rsem, to, first, count):
        return pltpu.make_async_remote_copy(
            src_ref=part_of(src, first, count), dst_ref=part_of(dst, first, count),
            send_sem=ssem, recv_sem=rsem,
            device_id={"expert": to}, device_id_type=MESH,
        )

    def send(first, last, src, dst, ssem, rsem, where):
        slots(first, last, lambda k: remote(src, dst, ssem, rsem, where(k), k, 1).start())

    def whole(first, last, src, dst, ssem, rsem):
        return remote(src, dst, ssem, rsem, ahead(1), first, last - first)

    inputs = [
        pltpu.make_async_copy(src, dst, in_sem.at[j])
        for j, (src, dst) in enumerate(
            (
                (be_hbm, be_ref), (live_hbm, live_ref), (tok_hbm, tok_ref),
                (prob_hbm, prob_ref), (go_hbm, go_ref),
            )
        )
    ]
    for load in inputs[:3]:
        load.start()
    barrier = pltpu.get_barrier_semaphore()
    slots(
        1, n,
        lambda k: pl.semaphore_signal(
            barrier, inc=1, device_id={"expert": ahead(k)}, device_id_type=MESH
        ),
    )
    for load in inputs[3:]:
        load.start()
    loads = [
        pltpu.make_async_copy(w_ref.at[0, 0], wcat.at[:, pl.ds(0, ff)], w_sem.at[0]),
        pltpu.make_async_copy(w_ref.at[0, 1], wcat.at[:, pl.ds(ff, ff)], w_sem.at[1]),
        pltpu.make_async_copy(w_ref.at[0, 2], wdown, w_sem.at[2]),
    ]
    for load in loads:
        load.start()

    def slot_of(expert):
        return (expert % half - place + half) % half + jnp.where(
            expert // half * half == side, 0, half
        )

    def keys(shape, axis):
        k = lax.broadcasted_iota(jnp.int32, shape, axis)
        part, row = k // rows, k % rows
        block, within = row // blk, row % blk
        owner = jnp.zeros(shape, jnp.int32)
        live = jnp.zeros(shape, jnp.int32)
        for b in range(nblk):
            owner = jnp.where(block == b, slot_of(be_ref[b]), owner)
            live = jnp.where(block == b, live_ref[b], live)
        return jnp.where(within < live, owner * SLOT + part * blk + within, -1)

    def stacked(value):
        return jnp.concatenate([value[:, p * pw:(p + 1) * pw] for p in range(parts)], axis=0)

    def one_hot(mask):
        return jnp.where(mask, 1.0, 0.0).astype(BF16)

    bulk = min(n, 16) * SLOT

    def pack(value, into):
        def step(c, carry):
            at = pl.multiple_of(c * bulk, bulk)
            ids = lax.broadcasted_iota(jnp.int32, (bulk, cols), 0) + c * bulk
            into[pl.ds(at, bulk), :] = dot(one_hot(ids == key_row), value).astype(BF16)
            return carry

        lax.fori_loop(0, n * SLOT // bulk, step, 0)

    for load in inputs[:3]:
        load.wait()
    key_row = keys((1, cols), 1)
    pack(stacked(tok_ref[...]), send_x)
    pl.semaphore_wait(barrier, n - 1)
    send(half, mid, send_x, got_x, sx_sem.at[0], rx_sem.at[0], ahead)
    send(1, half, send_x, got_x, sx_sem.at[0], rx_sem.at[0], ahead)

    for load in inputs[3:]:
        load.wait()
    probs = []
    for g in range(rows // lanes):
        square = (lanes, lanes)
        diagonal = lax.broadcasted_iota(jnp.int32, square, 0) == lax.broadcasted_iota(
            jnp.int32, square, 1
        )
        line = jnp.broadcast_to(prob_ref[g:g + 1, :], square)
        probs.append(jnp.sum(jnp.where(diagonal, line, 0.0), axis=1, keepdims=True))
    prob = jnp.concatenate(probs, axis=0) if len(probs) > 1 else probs[0]
    pack(stacked((prob * go_ref[...].astype(F32)).astype(BF16)), send_c)
    send(half, mid, send_c, got_c, sc_sem.at[0], rc_sem.at[0], ahead)
    send(1, half, send_c, got_c, sc_sem.at[0], rc_sem.at[0], ahead)
    send(mid, n, send_x, got_x, sx_sem.at[1], rx_sem.at[1], ahead)
    send(mid, n, send_c, got_c, sc_sem.at[1], rc_sem.at[1], ahead)
    got_x[:SLOT, :] = send_x[:SLOT, :]
    got_c[:SLOT, :] = send_c[:SLOT, :]

    key_column = keys((cols, 1), 0)

    def pick_back(c, carry):
        at = pl.multiple_of(c * bulk, bulk)
        ids = lax.broadcasted_iota(jnp.int32, (cols, bulk), 1) + c * bulk
        back_ref[:, pl.ds(at, bulk)] = one_hot(ids == key_column)
        return carry

    lax.fori_loop(0, n * SLOT // bulk, pick_back, 0)

    class Chunk:
        def __init__(self, first, last, count):
            self.first, self.last, self.count = first, last, count
            self.span, self.grow = count * SLOT, count * blk
            i = lax.broadcasted_iota(jnp.int32, (self.span, self.span), 0)
            k = lax.broadcasted_iota(jnp.int32, (self.span, self.span), 1)
            grow = self.grow
            self.unslot = one_hot(k == (i % grow) // blk * SLOT + i // grow * blk + i % blk)
            self.toslot = one_hot(i == (k % grow) // blk * SLOT + k // grow * blk + k % blk)

        def each(self, body):
            def step(c, carry):
                first = self.first + c * self.count
                body(
                    first,
                    pl.ds(pl.multiple_of(first * SLOT, SLOT), self.span),
                    pl.ds(pl.multiple_of(first * blk, SLOT), self.grow),
                )
                return carry

            lax.fori_loop(0, (self.last - self.first) // self.count, step, 0)

        def unpack(self, got, into):
            def body(first, slot_rows, here):
                value = dot(self.unslot, got[slot_rows, :]).astype(BF16)
                for p in range(parts):
                    into[here, p * pw:(p + 1) * pw] = value[p * self.grow:(p + 1) * self.grow, :]

            self.each(body)

        def forward(self):
            def body(first, slot_rows, here):
                both = dot(rows_x[here, :], wcat[...])
                gate, up = both[:, :ff], both[:, ff:]
                sigma = jax.nn.sigmoid(gate)
                active = gate * sigma
                hid[here, :] = (active * up).astype(BF16)
                d_cat[here, :ff] = up * sigma * (1.0 + gate * (1.0 - sigma))
                d_cat[here, ff:] = active

            self.each(body)

        def backward(self):
            def body(first, slot_rows, here):
                pulled = dot(rows_c[here, :], wdown[...])
                hidden = hid[here, :]
                share = jnp.sum(hidden.astype(F32) * pulled, axis=1, keepdims=True)
                share = jnp.broadcast_to(share, (self.grow, send_t.shape[2]))
                for j in range(self.count):
                    send_t[first + j] = share[j * blk:(j + 1) * blk, :]
                d_both = jnp.concatenate([pulled, pulled], axis=1) * d_cat[here, :]
                d_cat[here, :] = d_both
                d_in = dot(d_both.astype(BF16), wback[...]).astype(BF16)
                send_d[slot_rows, :] = dot(self.toslot, stacked(d_in)).astype(BF16)

            self.each(body)

    early, late = Chunk(0, mid, 3 * group), Chunk(mid, n, group)
    for load in loads:
        load.wait()
    for p in range(parts):
        wback[:, p * pw:(p + 1) * pw] = wcat[p * pw:(p + 1) * pw, :].T
    whole(1, mid, send_x, got_x, sx_sem.at[0], rx_sem.at[0]).wait_recv()
    early.unpack(got_x, rows_x)
    early.forward()
    whole(1, mid, send_c, got_c, sc_sem.at[0], rc_sem.at[0]).wait_recv()
    early.unpack(got_c, rows_c)
    early.backward()
    send(1, half, send_d, got_d, sd_sem, rd_sem, behind)
    got_d[:SLOT, :] = send_d[:SLOT, :]
    whole(mid, n, send_x, got_x, sx_sem.at[1], rx_sem.at[1]).wait_recv()
    late.unpack(got_x, rows_x)
    late.forward()
    whole(mid, n, send_c, got_c, sc_sem.at[1], rc_sem.at[1]).wait_recv()
    send(half, mid, send_d, got_d, sd_sem, rd_sem, behind)
    late.unpack(got_c, rows_c)
    late.backward()
    send(mid, n, send_d, got_d, sd_sem, rd_sem, behind)
    send(1, n, send_t, got_t, st_sem, rt_sem, behind)
    got_t[0] = send_t[0]

    d_all = d_cat[...].astype(BF16)
    for p in range(parts):
        here = pl.ds(p * pw, pw)
        grads = dot_tn(rows_x[:, here], d_all).astype(BF16)
        wg_ref[0, 0, here, :] = grads[:, :ff]
        wg_ref[0, 1, here, :] = grads[:, ff:]
        wg_ref[0, 2, here, :] = dot_tn(rows_c[:, here], hid[...]).astype(BF16)

    every_t = whole(1, n, send_t, got_t, st_sem, rt_sem)
    every_t.wait_recv()
    lane = lax.broadcasted_iota(jnp.int32, (blk, got_t.shape[2]), 1)
    row = lax.broadcasted_iota(jnp.int32, (blk, got_t.shape[2]), 0)
    per = lanes // blk
    for g in range(rows // lanes):
        line = jnp.zeros((blk, got_t.shape[2]), F32)
        for j in range(per):
            line = jnp.where(lane == j * blk + row, got_t[slot_of(be_ref[g * per + j])], line)
        total = jnp.sum(line, axis=0, keepdims=True)[:, :lanes]
        dprob_ref[g:g + 1, :] = total / prob_ref[g:g + 1, :]

    for j, (first, last) in enumerate(((1, mid), (mid, n))):
        whole(first, last, send_x, got_x, sx_sem.at[j], rx_sem.at[j]).wait_send()
        whole(first, last, send_c, got_c, sc_sem.at[j], rc_sem.at[j]).wait_send()
    every_t.wait_send()
    every_d = whole(1, n, send_d, got_d, sd_sem, rd_sem)
    every_d.wait_send()
    every_d.wait_recv()


def store_kernel(got_d, back, d_prob, wg, dtok_hbm, dprob_hbm, wg_hbm, d_tokens, sem):
    stores = [
        pltpu.make_async_copy(wg, wg_hbm, sem.at[0]),
        pltpu.make_async_copy(d_prob, dprob_hbm, sem.at[1]),
        pltpu.make_async_copy(d_tokens, dtok_hbm, sem.at[2]),
    ]
    stores[0].start()
    stores[1].start()
    rows = d_tokens.shape[0]
    pw = got_d.shape[1]
    parts = d_tokens.shape[1] // pw
    for p in range(parts):
        picked = dot(back[p * rows:(p + 1) * rows, :], got_d[...])
        d_tokens[:, p * pw:(p + 1) * pw] = picked.astype(BF16)
    stores[2].start()
    for store in stores:
        store.wait()


def shards(n, tokens, grad_out, route_prob, block_expert, block_live, expert_weights):
    rows, width = tokens.shape
    blk = rows // block_expert.shape[0]
    ff = expert_weights.shape[3]
    parts = SLOT // blk
    pw = width // parts
    group = min(n // 4, 4)
    lanes = min(rows, 128)
    slots = (n * SLOT, pw)
    every = n * blk
    vmem = pl.BlockSpec(memory_space=pltpu.VMEM)
    any_ = pl.BlockSpec(memory_space=pl.ANY)
    dma = pltpu.SemaphoreType.DMA
    shapes = (
        ((rows, width), BF16),
        ((rows // lanes, lanes), F32),
        ((1, 3, width, ff), BF16),
    )
    results = pl.pallas_call(
        functools.partial(kernel, n, blk, group),
        out_shape=(
            pltpu.VMEM(slots, BF16),
            pltpu.VMEM((parts * rows, n * SLOT), BF16),
            *[pltpu.VMEM(*shape) for shape in shapes[1:]],
        ),
        in_specs=[any_] * 6,
        out_specs=(vmem,) * 4,
        scratch_shapes=[
            pltpu.VMEM((rows, width), BF16),
            pltpu.VMEM((rows, width), BF16),
            pltpu.VMEM((rows // lanes, lanes), F32),
            pltpu.SMEM(block_expert.shape, jnp.int32),
            pltpu.SMEM(block_live.shape, jnp.int32),
            pltpu.VMEM((width, 2 * ff), BF16),
            pltpu.VMEM((2 * ff, width), BF16),
            pltpu.VMEM((width, ff), BF16),
            *[pltpu.VMEM(slots, BF16) for _ in range(5)],
            *[pltpu.VMEM((n, blk, 128), F32) for _ in range(2)],
            pltpu.VMEM((every, width), BF16),
            pltpu.VMEM((every, width), BF16),
            pltpu.VMEM((every, 2 * ff), F32),
            pltpu.VMEM((every, ff), BF16),
            dma((5,)),
            dma((3,)),
            *[dma((2,)) for _ in range(4)],
            *[dma for _ in range(4)],
        ],
        compiler_params=pltpu.CompilerParams(
            collective_id=0, has_side_effects=True, vmem_limit_bytes=40 * 1024 * 1024
        ),
        cost_estimate=pl.CostEstimate(
            flops=2 * every * width * ff * 8,
            bytes_accessed=2 * 3 * width * ff * 2,
            transcendentals=every * ff,
        ),
    )(
        *[
            pltpu.with_memory_space_constraint(value, pltpu.HBM)
            for value in (
                tokens, grad_out, route_prob.reshape(rows // lanes, lanes),
                block_expert, block_live, expert_weights,
            )
        ]
    )
    d_tokens, d_prob, weight_grads = pl.pallas_call(
        store_kernel,
        out_shape=tuple(jax.ShapeDtypeStruct(*shape) for shape in shapes),
        in_specs=[vmem] * 4,
        out_specs=(any_,) * 3,
        scratch_shapes=[pltpu.VMEM((rows, width), BF16), dma((3,))],
        compiler_params=pltpu.CompilerParams(vmem_limit_bytes=8 * 1024 * 1024),
    )(*results)
    return (d_tokens, d_prob.reshape(rows), weight_grads)


def solution(mesh):
    placed = (
        P(("groups", "expert"), None),
        P(("groups", "expert"), None),
        P(("groups", "expert")),
        P(("groups", "expert")),
        P(("groups", "expert")),
        P("expert", None, None, None),
    )
    return jax.shard_map(
        functools.partial(shards, mesh.shape["expert"]),
        mesh=mesh,
        in_specs=placed,
        out_specs=(
            P(("groups", "expert"), None),
            P(("groups", "expert")),
            P(("groups", "expert"), None, None, None),
        ),
        check_vma=False,
    )
```

```python
import functools

import jax
import jax.numpy as jnp
from jax import lax
from jax.experimental import pallas as pl
from jax.experimental.pallas import tpu as pltpu
from jax.sharding import PartitionSpec as P

MESH = pl.DeviceIdType.MESH
SLOT = 16
F32 = jnp.float32
BF16 = jnp.bfloat16


def dot(a, b):
    return jnp.dot(a, b, preferred_element_type=F32)


def dot_tn(a, b):
    return lax.dot_general(a, b, (((0,), (0,)), ((), ())), preferred_element_type=F32)


def kernel(
    n, blk, group,
    tok_hbm, go_hbm, prob_hbm, be_hbm, live_hbm, w_ref,
    got_d, back_ref, dprob_ref, wg_ref,
    tok_ref, go_ref, prob_ref, be_ref, live_ref, wcat, wback, wdown,
    send_x, send_c, got_x, got_c, send_d, send_t, got_t, rows_x, rows_c, d_cat, hid,
    in_sem, w_sem, sx_sem, rx_sem, sc_sem, rc_sem, sd_sem, rd_sem, st_sem, rt_sem,
):
    me = lax.axis_index("expert")
    rows, width = tok_ref.shape
    ff = wdown.shape[1]
    nblk = rows // blk
    parts = SLOT // blk
    pw = width // parts
    cols = parts * rows
    lanes = prob_ref.shape[1]
    half = n // 2
    mid = half + half // 2
    side = me // half * half
    place = me % half

    def ahead(k):
        base = jnp.where(k < half, side, half - side)
        return base + (place + k) % half

    def behind(k):
        base = jnp.where(k < half, side, half - side)
        return base + (place - k + n) % half

    def slots(first, last, body):
        def step(k, carry):
            body(k)
            return carry

        lax.fori_loop(first, last, step, 0)

    def part_of(ref, first, count):
        if len(ref.shape) == 3:
            return ref.at[pl.ds(first, count)]
        start = first * SLOT
        if not isinstance(first, int):
            start = pl.multiple_of(start, SLOT)
        return ref.at[pl.ds(start, count * SLOT), :]

    def remote(src, dst, ssem, rsem, to, first, count):
        return pltpu.make_async_remote_copy(
            src_ref=part_of(src, first, count), dst_ref=part_of(dst, first, count),
            send_sem=ssem, recv_sem=rsem,
            device_id={"expert": to}, device_id_type=MESH,
        )

    def send(first, last, src, dst, ssem, rsem, where):
        slots(first, last, lambda k: remote(src, dst, ssem, rsem, where(k), k, 1).start())

    def whole(first, last, src, dst, ssem, rsem):
        return remote(src, dst, ssem, rsem, ahead(1), first, last - first)

    inputs = [
        pltpu.make_async_copy(src, dst, in_sem.at[j])
        for j, (src, dst) in enumerate(
            (
                (be_hbm, be_ref), (live_hbm, live_ref), (tok_hbm, tok_ref),
                (prob_hbm, prob_ref), (go_hbm, go_ref),
            )
        )
    ]
    for load in inputs[:3]:
        load.start()
    barrier = pltpu.get_barrier_semaphore()
    slots(
        1, n,
        lambda k: pl.semaphore_signal(
            barrier, inc=1, device_id={"expert": ahead(k)}, device_id_type=MESH
        ),
    )
    for load in inputs[3:]:
        load.start()
    loads = [
        pltpu.make_async_copy(w_ref.at[0, 0], wcat.at[:, pl.ds(0, ff)], w_sem.at[0]),
        pltpu.make_async_copy(w_ref.at[0, 1], wcat.at[:, pl.ds(ff, ff)], w_sem.at[1]),
        pltpu.make_async_copy(w_ref.at[0, 2], wdown, w_sem.at[2]),
    ]
    for load in loads:
        load.start()

    def slot_of(expert):
        return (expert % half - place + half) % half + jnp.where(
            expert // half * half == side, 0, half
        )

    def keys(shape, axis):
        k = lax.broadcasted_iota(jnp.int32, shape, axis)
        part, row = k // rows, k % rows
        block, within = row // blk, row % blk
        owner = jnp.zeros(shape, jnp.int32)
        live = jnp.zeros(shape, jnp.int32)
        for b in range(nblk):
            owner = jnp.where(block == b, slot_of(be_ref[b]), owner)
            live = jnp.where(block == b, live_ref[b], live)
        return jnp.where(within < live, owner * SLOT + part * blk + within, -1)

    def stacked(value):
        return jnp.concatenate([value[:, p * pw:(p + 1) * pw] for p in range(parts)], axis=0)

    def one_hot(mask):
        return jnp.where(mask, 1.0, 0.0).astype(BF16)

    bulk = min(n, 16) * SLOT

    def pack(value, into):
        def step(c, carry):
            at = pl.multiple_of(c * bulk, bulk)
            ids = lax.broadcasted_iota(jnp.int32, (bulk, cols), 0) + c * bulk
            into[pl.ds(at, bulk), :] = dot(one_hot(ids == key_row), value).astype(BF16)
            return carry

        lax.fori_loop(0, n * SLOT // bulk, step, 0)

    for load in inputs[:3]:
        load.wait()
    key_row = keys((1, cols), 1)
    pack(stacked(tok_ref[...]), send_x)
    pl.semaphore_wait(barrier, n - 1)
    send(half, mid, send_x, got_x, sx_sem.at[0], rx_sem.at[0], ahead)
    send(1, half, send_x, got_x, sx_sem.at[0], rx_sem.at[0], ahead)

    for load in inputs[3:]:
        load.wait()
    probs = []
    for g in range(rows // lanes):
        square = (lanes, lanes)
        diagonal = lax.broadcasted_iota(jnp.int32, square, 0) == lax.broadcasted_iota(
            jnp.int32, square, 1
        )
        line = jnp.broadcast_to(prob_ref[g:g + 1, :], square)
        probs.append(jnp.sum(jnp.where(diagonal, line, 0.0), axis=1, keepdims=True))
    prob = jnp.concatenate(probs, axis=0) if len(probs) > 1 else probs[0]
    pack(stacked((prob * go_ref[...].astype(F32)).astype(BF16)), send_c)
    send(half, mid, send_c, got_c, sc_sem.at[0], rc_sem.at[0], ahead)
    send(1, half, send_c, got_c, sc_sem.at[0], rc_sem.at[0], ahead)
    send(mid, n, send_x, got_x, sx_sem.at[1], rx_sem.at[1], ahead)
    send(mid, n, send_c, got_c, sc_sem.at[1], rc_sem.at[1], ahead)
    got_x[:SLOT, :] = send_x[:SLOT, :]
    got_c[:SLOT, :] = send_c[:SLOT, :]

    key_column = keys((cols, 1), 0)

    def pick_back(c, carry):
        at = pl.multiple_of(c * bulk, bulk)
        ids = lax.broadcasted_iota(jnp.int32, (cols, bulk), 1) + c * bulk
        back_ref[:, pl.ds(at, bulk)] = one_hot(ids == key_column)
        return carry

    lax.fori_loop(0, n * SLOT // bulk, pick_back, 0)

    class Chunk:
        def __init__(self, first, last, count):
            self.first, self.last, self.count = first, last, count
            self.span, self.grow = count * SLOT, count * blk
            i = lax.broadcasted_iota(jnp.int32, (self.span, self.span), 0)
            k = lax.broadcasted_iota(jnp.int32, (self.span, self.span), 1)
            grow = self.grow
            self.unslot = one_hot(k == (i % grow) // blk * SLOT + i // grow * blk + i % blk)
            self.toslot = one_hot(i == (k % grow) // blk * SLOT + k // grow * blk + k % blk)

        def each(self, body):
            def step(c, carry):
                first = self.first + c * self.count
                body(
                    first,
                    pl.ds(pl.multiple_of(first * SLOT, SLOT), self.span),
                    pl.ds(pl.multiple_of(first * blk, SLOT), self.grow),
                )
                return carry

            lax.fori_loop(0, (self.last - self.first) // self.count, step, 0)

        def unpack(self, got, into):
            def body(first, slot_rows, here):
                value = dot(self.unslot, got[slot_rows, :]).astype(BF16)
                for p in range(parts):
                    into[here, p * pw:(p + 1) * pw] = value[p * self.grow:(p + 1) * self.grow, :]

            self.each(body)

        def forward(self):
            def body(first, slot_rows, here):
                both = dot(rows_x[here, :], wcat[...])
                gate, up = both[:, :ff], both[:, ff:]
                sigma = jax.nn.sigmoid(gate)
                active = gate * sigma
                hid[here, :] = (active * up).astype(BF16)
                d_cat[here, :ff] = up * sigma * (1.0 + gate * (1.0 - sigma))
                d_cat[here, ff:] = active

            self.each(body)

        def backward(self):
            def body(first, slot_rows, here):
                pulled = dot(rows_c[here, :], wdown[...])
                hidden = hid[here, :]
                share = jnp.sum(hidden.astype(F32) * pulled, axis=1, keepdims=True)
                wide = (self.grow, send_t.shape[2])
                lane = lax.broadcasted_iota(jnp.int32, wide, 1)
                row = lax.broadcasted_iota(jnp.int32, wide, 0)
                share = jnp.where(lane % blk == row % blk, jnp.broadcast_to(share, wide), 0.0)
                for j in range(self.count):
                    send_t[first + j] = jnp.sum(
                        share[j * blk:(j + 1) * blk, :], axis=0, keepdims=True
                    )
                d_both = jnp.concatenate([pulled, pulled], axis=1) * d_cat[here, :]
                d_cat[here, :] = d_both
                d_in = dot(d_both.astype(BF16), wback[...]).astype(BF16)
                send_d[slot_rows, :] = dot(self.toslot, stacked(d_in)).astype(BF16)

            self.each(body)

    early, late = Chunk(0, mid, 3 * group), Chunk(mid, n, group)
    for load in loads:
        load.wait()
    for p in range(parts):
        wback[:, p * pw:(p + 1) * pw] = wcat[p * pw:(p + 1) * pw, :].T
    whole(1, mid, send_x, got_x, sx_sem.at[0], rx_sem.at[0]).wait_recv()
    early.unpack(got_x, rows_x)
    early.forward()
    whole(1, mid, send_c, got_c, sc_sem.at[0], rc_sem.at[0]).wait_recv()
    early.unpack(got_c, rows_c)
    early.backward()
    send(1, half, send_d, got_d, sd_sem, rd_sem, behind)
    got_d[:SLOT, :] = send_d[:SLOT, :]
    whole(mid, n, send_x, got_x, sx_sem.at[1], rx_sem.at[1]).wait_recv()
    send(half, mid, send_d, got_d, sd_sem, rd_sem, behind)
    send(1, mid, send_t, got_t, st_sem, rt_sem, behind)
    late.unpack(got_x, rows_x)
    late.forward()
    whole(mid, n, send_c, got_c, sc_sem.at[1], rc_sem.at[1]).wait_recv()
    late.unpack(got_c, rows_c)
    late.backward()
    send(mid, n, send_d, got_d, sd_sem, rd_sem, behind)
    send(mid, n, send_t, got_t, st_sem, rt_sem, behind)
    got_t[0] = send_t[0]

    d_all = d_cat[...].astype(BF16)
    for p in range(parts):
        here = pl.ds(p * pw, pw)
        grads = dot_tn(rows_x[:, here], d_all).astype(BF16)
        wg_ref[0, 0, here, :] = grads[:, :ff]
        wg_ref[0, 1, here, :] = grads[:, ff:]
        wg_ref[0, 2, here, :] = dot_tn(rows_c[:, here], hid[...]).astype(BF16)

    every_t = whole(1, n, send_t, got_t, st_sem, rt_sem)
    every_t.wait_recv()
    lane = lax.broadcasted_iota(jnp.int32, (1, got_t.shape[2]), 1)
    per = lanes // blk
    for g in range(rows // lanes):
        line = jnp.zeros((1, got_t.shape[2]), F32)
        for j in range(per):
            line = jnp.where(lane // blk == j, got_t[slot_of(be_ref[g * per + j])], line)
        dprob_ref[g:g + 1, :] = line[:, :lanes] / prob_ref[g:g + 1, :]

    for j, (first, last) in enumerate(((1, mid), (mid, n))):
        whole(first, last, send_x, got_x, sx_sem.at[j], rx_sem.at[j]).wait_send()
        whole(first, last, send_c, got_c, sc_sem.at[j], rc_sem.at[j]).wait_send()
    every_t.wait_send()
    every_d = whole(1, n, send_d, got_d, sd_sem, rd_sem)
    every_d.wait_send()
    every_d.wait_recv()


def store_kernel(got_d, back, d_prob, wg, dtok_hbm, dprob_hbm, wg_hbm, d_tokens, sem):
    stores = [
        pltpu.make_async_copy(wg, wg_hbm, sem.at[0]),
        pltpu.make_async_copy(d_prob, dprob_hbm, sem.at[1]),
        pltpu.make_async_copy(d_tokens, dtok_hbm, sem.at[2]),
    ]
    stores[0].start()
    stores[1].start()
    rows = d_tokens.shape[0]
    pw = got_d.shape[1]
    parts = d_tokens.shape[1] // pw
    for p in range(parts):
        picked = dot(back[p * rows:(p + 1) * rows, :], got_d[...])
        d_tokens[:, p * pw:(p + 1) * pw] = picked.astype(BF16)
    stores[2].start()
    for store in stores:
        store.wait()


def shards(n, tokens, grad_out, route_prob, block_expert, block_live, expert_weights):
    rows, width = tokens.shape
    blk = rows // block_expert.shape[0]
    ff = expert_weights.shape[3]
    parts = SLOT // blk
    pw = width // parts
    group = min(n // 4, 4)
    lanes = min(rows, 128)
    slots = (n * SLOT, pw)
    every = n * blk
    vmem = pl.BlockSpec(memory_space=pltpu.VMEM)
    any_ = pl.BlockSpec(memory_space=pl.ANY)
    dma = pltpu.SemaphoreType.DMA
    shapes = (
        ((rows, width), BF16),
        ((rows // lanes, lanes), F32),
        ((1, 3, width, ff), BF16),
    )
    results = pl.pallas_call(
        functools.partial(kernel, n, blk, group),
        out_shape=(
            pltpu.VMEM(slots, BF16),
            pltpu.VMEM((parts * rows, n * SLOT), BF16),
            *[pltpu.VMEM(*shape) for shape in shapes[1:]],
        ),
        in_specs=[any_] * 6,
        out_specs=(vmem,) * 4,
        scratch_shapes=[
            pltpu.VMEM((rows, width), BF16),
            pltpu.VMEM((rows, width), BF16),
            pltpu.VMEM((rows // lanes, lanes), F32),
            pltpu.SMEM(block_expert.shape, jnp.int32),
            pltpu.SMEM(block_live.shape, jnp.int32),
            pltpu.VMEM((width, 2 * ff), BF16),
            pltpu.VMEM((2 * ff, width), BF16),
            pltpu.VMEM((width, ff), BF16),
            *[pltpu.VMEM(slots, BF16) for _ in range(5)],
            *[pltpu.VMEM((n, 1, 128), F32) for _ in range(2)],
            pltpu.VMEM((every, width), BF16),
            pltpu.VMEM((every, width), BF16),
            pltpu.VMEM((every, 2 * ff), F32),
            pltpu.VMEM((every, ff), BF16),
            dma((5,)),
            dma((3,)),
            *[dma((2,)) for _ in range(4)],
            *[dma for _ in range(4)],
        ],
        compiler_params=pltpu.CompilerParams(
            collective_id=0, has_side_effects=True, vmem_limit_bytes=40 * 1024 * 1024
        ),
        cost_estimate=pl.CostEstimate(
            flops=2 * every * width * ff * 8,
            bytes_accessed=2 * 3 * width * ff * 2,
            transcendentals=every * ff,
        ),
    )(
        *[
            pltpu.with_memory_space_constraint(value, pltpu.HBM)
            for value in (
                tokens, grad_out, route_prob.reshape(rows // lanes, lanes),
                block_expert, block_live, expert_weights,
            )
        ]
    )
    d_tokens, d_prob, weight_grads = pl.pallas_call(
        store_kernel,
        out_shape=tuple(jax.ShapeDtypeStruct(*shape) for shape in shapes),
        in_specs=[vmem] * 4,
        out_specs=(any_,) * 3,
        scratch_shapes=[pltpu.VMEM((rows, width), BF16), dma((3,))],
        compiler_params=pltpu.CompilerParams(vmem_limit_bytes=8 * 1024 * 1024),
    )(*results)
    return (d_tokens, d_prob.reshape(rows), weight_grads)


def solution(mesh):
    placed = (
        P(("groups", "expert"), None),
        P(("groups", "expert"), None),
        P(("groups", "expert")),
        P(("groups", "expert")),
        P(("groups", "expert")),
        P("expert", None, None, None),
    )
    return jax.shard_map(
        functools.partial(shards, mesh.shape["expert"]),
        mesh=mesh,
        in_specs=placed,
        out_specs=(
            P(("groups", "expert"), None),
            P(("groups", "expert")),
            P(("groups", "expert"), None, None, None),
        ),
        check_vma=False,
    )
```

```python
import functools

import jax
import jax.numpy as jnp
from jax import lax
from jax.experimental import pallas as pl
from jax.experimental.pallas import tpu as pltpu
from jax.sharding import PartitionSpec as P

MESH = pl.DeviceIdType.MESH
SLOT = 16
F32 = jnp.float32
BF16 = jnp.bfloat16


def dot(a, b):
    return jnp.dot(a, b, preferred_element_type=F32)


def dot_tn(a, b):
    return lax.dot_general(a, b, (((0,), (0,)), ((), ())), preferred_element_type=F32)


def kernel(
    n, blk, group,
    tok_hbm, go_hbm, prob_hbm, be_hbm, live_hbm, w_ref,
    got_d, back_ref, dprob_ref, wg_ref,
    tok_ref, go_ref, prob_ref, be_ref, live_ref, wcat, wback, wdown,
    send_x, send_c, got_x, got_c, send_d, send_t, got_t, rows_x, rows_c, d_cat, hid,
    in_sem, w_sem, sx_sem, rx_sem, sc_sem, rc_sem, sd_sem, rd_sem, st_sem, rt_sem,
):
    me = lax.axis_index("expert")
    rows, width = tok_ref.shape
    ff = wdown.shape[1]
    nblk = rows // blk
    parts = SLOT // blk
    pw = width // parts
    cols = parts * rows
    lanes = prob_ref.shape[1]
    half = n // 2
    mid = half + half // 2
    side = me // half * half
    place = me % half

    def base(k):
        if isinstance(k, int):
            return side if k < half else half - side
        return jnp.where(k < half, side, half - side)

    def ahead(k):
        return base(k) + (place + k) % half

    def behind(k):
        return base(k) + (place - k + n) % half

    def slots(first, last, body):
        def step(k, carry):
            body(k)
            return carry

        if last - first <= 16:
            for k in range(first, last):
                body(k)
        else:
            lax.fori_loop(first, last, step, 0)

    def part_of(ref, first, count):
        if len(ref.shape) == 3:
            return ref.at[pl.ds(first, count)]
        start = first * SLOT
        if not isinstance(first, int):
            start = pl.multiple_of(start, SLOT)
        return ref.at[pl.ds(start, count * SLOT), :]

    def remote(src, dst, ssem, rsem, to, first, count):
        return pltpu.make_async_remote_copy(
            src_ref=part_of(src, first, count), dst_ref=part_of(dst, first, count),
            send_sem=ssem, recv_sem=rsem,
            device_id={"expert": to}, device_id_type=MESH,
        )

    def send(first, last, src, dst, ssem, rsem, where):
        slots(first, last, lambda k: remote(src, dst, ssem, rsem, where(k), k, 1).start())

    def whole(first, last, src, dst, ssem, rsem):
        return remote(src, dst, ssem, rsem, ahead(1), first, last - first)

    inputs = [
        pltpu.make_async_copy(src, dst, in_sem.at[j])
        for j, (src, dst) in enumerate(
            (
                (be_hbm, be_ref), (live_hbm, live_ref), (tok_hbm, tok_ref),
                (prob_hbm, prob_ref), (go_hbm, go_ref),
            )
        )
    ]
    for load in inputs[:3]:
        load.start()
    barrier = pltpu.get_barrier_semaphore()
    slots(
        1, n,
        lambda k: pl.semaphore_signal(
            barrier, inc=1, device_id={"expert": ahead(k)}, device_id_type=MESH
        ),
    )
    for load in inputs[3:]:
        load.start()
    loads = [
        pltpu.make_async_copy(w_ref.at[0, 0], wcat.at[:, pl.ds(0, ff)], w_sem.at[0]),
        pltpu.make_async_copy(w_ref.at[0, 1], wcat.at[:, pl.ds(ff, ff)], w_sem.at[1]),
        pltpu.make_async_copy(w_ref.at[0, 2], wdown, w_sem.at[2]),
    ]
    for load in loads:
        load.start()

    def slot_of(expert):
        return (expert % half - place + half) % half + jnp.where(
            expert // half * half == side, 0, half
        )

    def keys(shape, axis):
        k = lax.broadcasted_iota(jnp.int32, shape, axis)
        part, row = k // rows, k % rows
        block, within = row // blk, row % blk
        owner = jnp.zeros(shape, jnp.int32)
        live = jnp.zeros(shape, jnp.int32)
        for b in range(nblk):
            owner = jnp.where(block == b, slot_of(be_ref[b]), owner)
            live = jnp.where(block == b, live_ref[b], live)
        return jnp.where(within < live, owner * SLOT + part * blk + within, -1)

    def stacked(value):
        return jnp.concatenate([value[:, p * pw:(p + 1) * pw] for p in range(parts)], axis=0)

    def one_hot(mask):
        return jnp.where(mask, 1.0, 0.0).astype(BF16)

    bulk = min(n, 16) * SLOT

    def pack(value, into):
        def step(c, carry):
            at = pl.multiple_of(c * bulk, bulk)
            ids = lax.broadcasted_iota(jnp.int32, (bulk, cols), 0) + c * bulk
            into[pl.ds(at, bulk), :] = dot(one_hot(ids == key_row), value).astype(BF16)
            return carry

        lax.fori_loop(0, n * SLOT // bulk, step, 0)

    for load in inputs[:3]:
        load.wait()
    key_row = keys((1, cols), 1)
    pack(stacked(tok_ref[...]), send_x)
    pl.semaphore_wait(barrier, n - 1)
    send(half, mid, send_x, got_x, sx_sem.at[0], rx_sem.at[0], ahead)
    send(1, half, send_x, got_x, sx_sem.at[0], rx_sem.at[0], ahead)

    for load in inputs[3:]:
        load.wait()
    probs = []
    for g in range(rows // lanes):
        square = (lanes, lanes)
        diagonal = lax.broadcasted_iota(jnp.int32, square, 0) == lax.broadcasted_iota(
            jnp.int32, square, 1
        )
        line = jnp.broadcast_to(prob_ref[g:g + 1, :], square)
        probs.append(jnp.sum(jnp.where(diagonal, line, 0.0), axis=1, keepdims=True))
    prob = jnp.concatenate(probs, axis=0) if len(probs) > 1 else probs[0]
    pack(stacked((prob * go_ref[...].astype(F32)).astype(BF16)), send_c)
    send(half, mid, send_c, got_c, sc_sem.at[0], rc_sem.at[0], ahead)
    send(1, half, send_c, got_c, sc_sem.at[0], rc_sem.at[0], ahead)
    send(mid, n, send_x, got_x, sx_sem.at[1], rx_sem.at[1], ahead)
    send(mid, n, send_c, got_c, sc_sem.at[1], rc_sem.at[1], ahead)
    got_x[:SLOT, :] = send_x[:SLOT, :]
    got_c[:SLOT, :] = send_c[:SLOT, :]

    key_column = keys((cols, 1), 0)

    def pick_back(c, carry):
        at = pl.multiple_of(c * bulk, bulk)
        ids = lax.broadcasted_iota(jnp.int32, (cols, bulk), 1) + c * bulk
        back_ref[:, pl.ds(at, bulk)] = one_hot(ids == key_column)
        return carry

    lax.fori_loop(0, n * SLOT // bulk, pick_back, 0)

    class Chunk:
        def __init__(self, first, last, count):
            self.first, self.last, self.count = first, last, count
            self.span, self.grow = count * SLOT, count * blk
            i = lax.broadcasted_iota(jnp.int32, (self.span, self.span), 0)
            k = lax.broadcasted_iota(jnp.int32, (self.span, self.span), 1)
            grow = self.grow
            self.unslot = one_hot(k == (i % grow) // blk * SLOT + i // grow * blk + i % blk)
            self.toslot = one_hot(i == (k % grow) // blk * SLOT + k // grow * blk + k % blk)

        def each(self, body):
            def step(c, carry):
                first = self.first + c * self.count
                body(
                    first,
                    pl.ds(pl.multiple_of(first * SLOT, SLOT), self.span),
                    pl.ds(pl.multiple_of(first * blk, SLOT), self.grow),
                )
                return carry

            lax.fori_loop(0, (self.last - self.first) // self.count, step, 0)

        def unpack(self, got, into):
            def body(first, slot_rows, here):
                value = dot(self.unslot, got[slot_rows, :]).astype(BF16)
                for p in range(parts):
                    into[here, p * pw:(p + 1) * pw] = value[p * self.grow:(p + 1) * self.grow, :]

            self.each(body)

        def forward(self):
            def body(first, slot_rows, here):
                both = dot(rows_x[here, :], wcat[...])
                gate, up = both[:, :ff], both[:, ff:]
                sigma = jax.nn.sigmoid(gate)
                active = gate * sigma
                hid[here, :] = (active * up).astype(BF16)
                d_cat[here, :ff] = up * sigma * (1.0 + gate * (1.0 - sigma))
                d_cat[here, ff:] = active

            self.each(body)

        def backward(self):
            def body(first, slot_rows, here):
                pulled = dot(rows_c[here, :], wdown[...])
                hidden = hid[here, :]
                share = jnp.sum(hidden.astype(F32) * pulled, axis=1, keepdims=True)
                wide = (self.grow, send_t.shape[2])
                lane = lax.broadcasted_iota(jnp.int32, wide, 1)
                row = lax.broadcasted_iota(jnp.int32, wide, 0)
                share = jnp.where(lane % blk == row % blk, jnp.broadcast_to(share, wide), 0.0)
                for j in range(self.count):
                    send_t[first + j] = jnp.sum(
                        share[j * blk:(j + 1) * blk, :], axis=0, keepdims=True
                    )
                d_both = jnp.concatenate([pulled, pulled], axis=1) * d_cat[here, :]
                d_cat[here, :] = d_both
                d_in = dot(d_both.astype(BF16), wback[...]).astype(BF16)
                send_d[slot_rows, :] = dot(self.toslot, stacked(d_in)).astype(BF16)

            self.each(body)

    early, late = Chunk(0, mid, 3 * group), Chunk(mid, n, group)
    for load in loads:
        load.wait()
    for p in range(parts):
        wback[:, p * pw:(p + 1) * pw] = wcat[p * pw:(p + 1) * pw, :].T
    whole(1, mid, send_x, got_x, sx_sem.at[0], rx_sem.at[0]).wait_recv()
    early.unpack(got_x, rows_x)
    early.forward()
    whole(1, mid, send_c, got_c, sc_sem.at[0], rc_sem.at[0]).wait_recv()
    early.unpack(got_c, rows_c)
    early.backward()
    send(half, mid, send_d, got_d, sd_sem, rd_sem, behind)
    send(1, half, send_d, got_d, sd_sem, rd_sem, behind)
    send(1, mid, send_t, got_t, st_sem, rt_sem, behind)
    got_d[:SLOT, :] = send_d[:SLOT, :]
    whole(mid, n, send_x, got_x, sx_sem.at[1], rx_sem.at[1]).wait_recv()
    late.unpack(got_x, rows_x)
    late.forward()
    whole(mid, n, send_c, got_c, sc_sem.at[1], rc_sem.at[1]).wait_recv()
    late.unpack(got_c, rows_c)
    late.backward()
    send(mid, n, send_d, got_d, sd_sem, rd_sem, behind)
    send(mid, n, send_t, got_t, st_sem, rt_sem, behind)
    got_t[0] = send_t[0]

    d_all = d_cat[...].astype(BF16)
    for p in range(parts):
        here = pl.ds(p * pw, pw)
        grads = dot_tn(rows_x[:, here], d_all).astype(BF16)
        wg_ref[0, 0, here, :] = grads[:, :ff]
        wg_ref[0, 1, here, :] = grads[:, ff:]
        wg_ref[0, 2, here, :] = dot_tn(rows_c[:, here], hid[...]).astype(BF16)

    every_t = whole(1, n, send_t, got_t, st_sem, rt_sem)
    every_t.wait_recv()
    lane = lax.broadcasted_iota(jnp.int32, (1, got_t.shape[2]), 1)
    per = lanes // blk
    for g in range(rows // lanes):
        line = jnp.zeros((1, got_t.shape[2]), F32)
        for j in range(per):
            line = jnp.where(lane // blk == j, got_t[slot_of(be_ref[g * per + j])], line)
        dprob_ref[g:g + 1, :] = line[:, :lanes] / prob_ref[g:g + 1, :]

    for j, (first, last) in enumerate(((1, mid), (mid, n))):
        whole(first, last, send_x, got_x, sx_sem.at[j], rx_sem.at[j]).wait_send()
        whole(first, last, send_c, got_c, sc_sem.at[j], rc_sem.at[j]).wait_send()
    every_t.wait_send()
    every_d = whole(1, n, send_d, got_d, sd_sem, rd_sem)
    every_d.wait_send()
    every_d.wait_recv()


def store_kernel(got_d, back, d_prob, wg, dtok_hbm, dprob_hbm, wg_hbm, d_tokens, sem):
    stores = [
        pltpu.make_async_copy(wg, wg_hbm, sem.at[0]),
        pltpu.make_async_copy(d_prob, dprob_hbm, sem.at[1]),
        pltpu.make_async_copy(d_tokens, dtok_hbm, sem.at[2]),
    ]
    stores[0].start()
    stores[1].start()
    rows = d_tokens.shape[0]
    pw = got_d.shape[1]
    parts = d_tokens.shape[1] // pw
    for p in range(parts):
        picked = dot(back[p * rows:(p + 1) * rows, :], got_d[...])
        d_tokens[:, p * pw:(p + 1) * pw] = picked.astype(BF16)
    stores[2].start()
    for store in stores:
        store.wait()


def shards(n, tokens, grad_out, route_prob, block_expert, block_live, expert_weights):
    rows, width = tokens.shape
    blk = rows // block_expert.shape[0]
    ff = expert_weights.shape[3]
    parts = SLOT // blk
    pw = width // parts
    group = min(n // 4, 4)
    lanes = min(rows, 128)
    slots = (n * SLOT, pw)
    every = n * blk
    vmem = pl.BlockSpec(memory_space=pltpu.VMEM)
    any_ = pl.BlockSpec(memory_space=pl.ANY)
    dma = pltpu.SemaphoreType.DMA
    shapes = (
        ((rows, width), BF16),
        ((rows // lanes, lanes), F32),
        ((1, 3, width, ff), BF16),
    )
    results = pl.pallas_call(
        functools.partial(kernel, n, blk, group),
        out_shape=(
            pltpu.VMEM(slots, BF16),
            pltpu.VMEM((parts * rows, n * SLOT), BF16),
            *[pltpu.VMEM(*shape) for shape in shapes[1:]],
        ),
        in_specs=[any_] * 6,
        out_specs=(vmem,) * 4,
        scratch_shapes=[
            pltpu.VMEM((rows, width), BF16),
            pltpu.VMEM((rows, width), BF16),
            pltpu.VMEM((rows // lanes, lanes), F32),
            pltpu.SMEM(block_expert.shape, jnp.int32),
            pltpu.SMEM(block_live.shape, jnp.int32),
            pltpu.VMEM((width, 2 * ff), BF16),
            pltpu.VMEM((2 * ff, width), BF16),
            pltpu.VMEM((width, ff), BF16),
            *[pltpu.VMEM(slots, BF16) for _ in range(5)],
            *[pltpu.VMEM((n, 1, 128), F32) for _ in range(2)],
            pltpu.VMEM((every, width), BF16),
            pltpu.VMEM((every, width), BF16),
            pltpu.VMEM((every, 2 * ff), F32),
            pltpu.VMEM((every, ff), BF16),
            dma((5,)),
            dma((3,)),
            *[dma((2,)) for _ in range(4)],
            *[dma for _ in range(4)],
        ],
        compiler_params=pltpu.CompilerParams(
            collective_id=0, has_side_effects=True, vmem_limit_bytes=40 * 1024 * 1024
        ),
        cost_estimate=pl.CostEstimate(
            flops=2 * every * width * ff * 8,
            bytes_accessed=2 * 3 * width * ff * 2,
            transcendentals=every * ff,
        ),
    )(
        *[
            pltpu.with_memory_space_constraint(value, pltpu.HBM)
            for value in (
                tokens, grad_out, route_prob.reshape(rows // lanes, lanes),
                block_expert, block_live, expert_weights,
            )
        ]
    )
    d_tokens, d_prob, weight_grads = pl.pallas_call(
        store_kernel,
        out_shape=tuple(jax.ShapeDtypeStruct(*shape) for shape in shapes),
        in_specs=[vmem] * 4,
        out_specs=(any_,) * 3,
        scratch_shapes=[pltpu.VMEM((rows, width), BF16), dma((3,))],
        compiler_params=pltpu.CompilerParams(vmem_limit_bytes=8 * 1024 * 1024),
    )(*results)
    return (d_tokens, d_prob.reshape(rows), weight_grads)


def solution(mesh):
    placed = (
        P(("groups", "expert"), None),
        P(("groups", "expert"), None),
        P(("groups", "expert")),
        P(("groups", "expert")),
        P(("groups", "expert")),
        P("expert", None, None, None),
    )
    return jax.shard_map(
        functools.partial(shards, mesh.shape["expert"]),
        mesh=mesh,
        in_specs=placed,
        out_specs=(
            P(("groups", "expert"), None),
            P(("groups", "expert")),
            P(("groups", "expert"), None, None, None),
        ),
        check_vma=False,
    )
```

```python
import functools

import jax
import jax.numpy as jnp
from jax import lax
from jax.experimental import pallas as pl
from jax.experimental.pallas import tpu as pltpu
from jax.sharding import PartitionSpec as P

MESH = pl.DeviceIdType.MESH
SLOT = 16
F32 = jnp.float32
BF16 = jnp.bfloat16


def dot(a, b):
    return jnp.dot(a, b, preferred_element_type=F32)


def dot_tn(a, b):
    return lax.dot_general(a, b, (((0,), (0,)), ((), ())), preferred_element_type=F32)


def kernel(
    n, blk, group,
    tok_hbm, go_hbm, prob_hbm, be_hbm, live_hbm, w_ref,
    got_d, back_ref, dprob_ref, wg_ref,
    tok_ref, go_ref, prob_ref, be_ref, live_ref, wcat, wback, wdown,
    send_x, send_c, got_x, got_c, send_d, send_t, got_t, rows_x, rows_c, d_cat, hid,
    in_sem, w_sem, sx_sem, rx_sem, sc_sem, rc_sem, sd_sem, rd_sem, st_sem, rt_sem,
):
    me = lax.axis_index("expert")
    rows, width = tok_ref.shape
    ff = wdown.shape[1]
    nblk = rows // blk
    parts = SLOT // blk
    pw = width // parts
    cols = parts * rows
    lanes = prob_ref.shape[1]
    half = n // 2
    mid = half + half // 2
    side = me // half * half
    place = me % half

    def base(k):
        if isinstance(k, int):
            return side if k < half else half - side
        return jnp.where(k < half, side, half - side)

    def ahead(k):
        return base(k) + (place + k) % half

    def behind(k):
        return base(k) + (place - k + n) % half

    def slots(first, last, body):
        def step(k, carry):
            body(k)
            return carry

        if last - first <= 16:
            for k in range(first, last):
                body(k)
        else:
            lax.fori_loop(first, last, step, 0)

    def part_of(ref, first, count):
        if len(ref.shape) == 3:
            return ref.at[pl.ds(first, count)]
        start = first * SLOT
        if not isinstance(first, int):
            start = pl.multiple_of(start, SLOT)
        return ref.at[pl.ds(start, count * SLOT), :]

    def remote(src, dst, ssem, rsem, to, first, count):
        return pltpu.make_async_remote_copy(
            src_ref=part_of(src, first, count), dst_ref=part_of(dst, first, count),
            send_sem=ssem, recv_sem=rsem,
            device_id={"expert": to}, device_id_type=MESH,
        )

    def send(first, last, src, dst, ssem, rsem, where):
        slots(first, last, lambda k: remote(src, dst, ssem, rsem, where(k), k, 1).start())

    def whole(first, last, src, dst, ssem, rsem):
        return remote(src, dst, ssem, rsem, ahead(1), first, last - first)

    inputs = [
        pltpu.make_async_copy(src, dst, in_sem.at[j])
        for j, (src, dst) in enumerate(
            (
                (be_hbm, be_ref), (live_hbm, live_ref), (tok_hbm, tok_ref),
                (prob_hbm, prob_ref), (go_hbm, go_ref),
            )
        )
    ]
    for load in inputs[:3]:
        load.start()
    barrier = pltpu.get_barrier_semaphore()
    slots(
        1, n,
        lambda k: pl.semaphore_signal(
            barrier, inc=1, device_id={"expert": ahead(k)}, device_id_type=MESH
        ),
    )
    for load in inputs[3:]:
        load.start()
    loads = [
        pltpu.make_async_copy(w_ref.at[0, 0], wcat.at[:, pl.ds(0, ff)], w_sem.at[0]),
        pltpu.make_async_copy(w_ref.at[0, 1], wcat.at[:, pl.ds(ff, ff)], w_sem.at[1]),
        pltpu.make_async_copy(w_ref.at[0, 2], wdown, w_sem.at[2]),
    ]
    for load in loads:
        load.start()

    def slot_of(expert):
        return (expert % half - place + half) % half + jnp.where(
            expert // half * half == side, 0, half
        )

    def keys(shape, axis):
        k = lax.broadcasted_iota(jnp.int32, shape, axis)
        part, row = k // rows, k % rows
        block, within = row // blk, row % blk
        owner = jnp.zeros(shape, jnp.int32)
        live = jnp.zeros(shape, jnp.int32)
        for b in range(nblk):
            owner = jnp.where(block == b, slot_of(be_ref[b]), owner)
            live = jnp.where(block == b, live_ref[b], live)
        return jnp.where(within < live, owner * SLOT + part * blk + within, -1)

    def stacked(value):
        return jnp.concatenate([value[:, p * pw:(p + 1) * pw] for p in range(parts)], axis=0)

    def one_hot(mask):
        return jnp.where(mask, 1.0, 0.0).astype(BF16)

    bulk = min(n, 16) * SLOT

    few = group * SLOT

    def pack(first, last, value, into):
        def step(c, carry):
            at = pl.multiple_of(first * SLOT + c * few, SLOT)
            ids = lax.broadcasted_iota(jnp.int32, (few, cols), 0) + at
            into[pl.ds(at, few), :] = dot(one_hot(ids == key_row), value).astype(BF16)
            return carry

        lax.fori_loop(0, (last - first) // group, step, 0)

    for load in inputs[:3]:
        load.wait()
    key_row = keys((1, cols), 1)
    tok4 = stacked(tok_ref[...])
    pack(half, mid, tok4, send_x)
    pl.semaphore_wait(barrier, n - 1)
    send(half, mid, send_x, got_x, sx_sem.at[0], rx_sem.at[0], ahead)
    pack(0, half, tok4, send_x)
    send(1, half, send_x, got_x, sx_sem.at[0], rx_sem.at[0], ahead)

    for load in inputs[3:]:
        load.wait()
    probs = []
    for g in range(rows // lanes):
        square = (lanes, lanes)
        diagonal = lax.broadcasted_iota(jnp.int32, square, 0) == lax.broadcasted_iota(
            jnp.int32, square, 1
        )
        line = jnp.broadcast_to(prob_ref[g:g + 1, :], square)
        probs.append(jnp.sum(jnp.where(diagonal, line, 0.0), axis=1, keepdims=True))
    prob = jnp.concatenate(probs, axis=0) if len(probs) > 1 else probs[0]
    cot4 = stacked((prob * go_ref[...].astype(F32)).astype(BF16))
    pack(half, mid, cot4, send_c)
    send(half, mid, send_c, got_c, sc_sem.at[0], rc_sem.at[0], ahead)
    pack(0, half, cot4, send_c)
    send(1, half, send_c, got_c, sc_sem.at[0], rc_sem.at[0], ahead)
    pack(mid, n, tok4, send_x)
    send(mid, n, send_x, got_x, sx_sem.at[1], rx_sem.at[1], ahead)
    pack(mid, n, cot4, send_c)
    send(mid, n, send_c, got_c, sc_sem.at[1], rc_sem.at[1], ahead)
    got_x[:SLOT, :] = send_x[:SLOT, :]
    got_c[:SLOT, :] = send_c[:SLOT, :]

    key_column = keys((cols, 1), 0)

    def pick_back(c, carry):
        at = pl.multiple_of(c * bulk, bulk)
        ids = lax.broadcasted_iota(jnp.int32, (cols, bulk), 1) + c * bulk
        back_ref[:, pl.ds(at, bulk)] = one_hot(ids == key_column)
        return carry

    lax.fori_loop(0, n * SLOT // bulk, pick_back, 0)

    class Chunk:
        def __init__(self, first, last, count):
            self.first, self.last, self.count = first, last, count
            self.span, self.grow = count * SLOT, count * blk
            i = lax.broadcasted_iota(jnp.int32, (self.span, self.span), 0)
            k = lax.broadcasted_iota(jnp.int32, (self.span, self.span), 1)
            grow = self.grow
            self.unslot = one_hot(k == (i % grow) // blk * SLOT + i // grow * blk + i % blk)
            self.toslot = one_hot(i == (k % grow) // blk * SLOT + k // grow * blk + k % blk)

        def each(self, body):
            def step(c, carry):
                first = self.first + c * self.count
                body(
                    first,
                    pl.ds(pl.multiple_of(first * SLOT, SLOT), self.span),
                    pl.ds(pl.multiple_of(first * blk, SLOT), self.grow),
                )
                return carry

            lax.fori_loop(0, (self.last - self.first) // self.count, step, 0)

        def unpack(self, got, into):
            def body(first, slot_rows, here):
                value = dot(self.unslot, got[slot_rows, :]).astype(BF16)
                for p in range(parts):
                    into[here, p * pw:(p + 1) * pw] = value[p * self.grow:(p + 1) * self.grow, :]

            self.each(body)

        def forward(self):
            def body(first, slot_rows, here):
                both = dot(rows_x[here, :], wcat[...])
                gate, up = both[:, :ff], both[:, ff:]
                sigma = jax.nn.sigmoid(gate)
                active = gate * sigma
                hid[here, :] = (active * up).astype(BF16)
                d_cat[here, :ff] = up * sigma * (1.0 + gate * (1.0 - sigma))
                d_cat[here, ff:] = active

            self.each(body)

        def backward(self):
            def body(first, slot_rows, here):
                pulled = dot(rows_c[here, :], wdown[...])
                hidden = hid[here, :]
                share = jnp.sum(hidden.astype(F32) * pulled, axis=1, keepdims=True)
                wide = (self.grow, send_t.shape[2])
                lane = lax.broadcasted_iota(jnp.int32, wide, 1)
                row = lax.broadcasted_iota(jnp.int32, wide, 0)
                share = jnp.where(lane % blk == row % blk, jnp.broadcast_to(share, wide), 0.0)
                for j in range(self.count):
                    send_t[first + j] = jnp.sum(
                        share[j * blk:(j + 1) * blk, :], axis=0, keepdims=True
                    )
                d_both = jnp.concatenate([pulled, pulled], axis=1) * d_cat[here, :]
                d_cat[here, :] = d_both
                d_in = dot(d_both.astype(BF16), wback[...]).astype(BF16)
                send_d[slot_rows, :] = dot(self.toslot, stacked(d_in)).astype(BF16)

            self.each(body)

    early, late = Chunk(0, mid, 3 * group), Chunk(mid, n, group)
    for load in loads:
        load.wait()
    for p in range(parts):
        wback[:, p * pw:(p + 1) * pw] = wcat[p * pw:(p + 1) * pw, :].T
    whole(1, mid, send_x, got_x, sx_sem.at[0], rx_sem.at[0]).wait_recv()
    early.unpack(got_x, rows_x)
    early.forward()
    whole(1, mid, send_c, got_c, sc_sem.at[0], rc_sem.at[0]).wait_recv()
    early.unpack(got_c, rows_c)
    early.backward()
    send(1, half, send_d, got_d, sd_sem, rd_sem, behind)
    got_d[:SLOT, :] = send_d[:SLOT, :]
    whole(mid, n, send_x, got_x, sx_sem.at[1], rx_sem.at[1]).wait_recv()
    send(half, mid, send_d, got_d, sd_sem, rd_sem, behind)
    send(1, mid, send_t, got_t, st_sem, rt_sem, behind)
    late.unpack(got_x, rows_x)
    late.forward()
    whole(mid, n, send_c, got_c, sc_sem.at[1], rc_sem.at[1]).wait_recv()
    late.unpack(got_c, rows_c)
    late.backward()
    send(mid, n, send_d, got_d, sd_sem, rd_sem, behind)
    send(mid, n, send_t, got_t, st_sem, rt_sem, behind)
    got_t[0] = send_t[0]

    d_all = d_cat[...].astype(BF16)
    for p in range(parts):
        here = pl.ds(p * pw, pw)
        grads = dot_tn(rows_x[:, here], d_all).astype(BF16)
        wg_ref[0, 0, here, :] = grads[:, :ff]
        wg_ref[0, 1, here, :] = grads[:, ff:]
        wg_ref[0, 2, here, :] = dot_tn(rows_c[:, here], hid[...]).astype(BF16)

    every_t = whole(1, n, send_t, got_t, st_sem, rt_sem)
    every_t.wait_recv()
    lane = lax.broadcasted_iota(jnp.int32, (1, got_t.shape[2]), 1)
    per = lanes // blk
    for g in range(rows // lanes):
        line = jnp.zeros((1, got_t.shape[2]), F32)
        for j in range(per):
            line = jnp.where(lane // blk == j, got_t[slot_of(be_ref[g * per + j])], line)
        dprob_ref[g:g + 1, :] = line[:, :lanes] / prob_ref[g:g + 1, :]

    for j, (first, last) in enumerate(((1, mid), (mid, n))):
        whole(first, last, send_x, got_x, sx_sem.at[j], rx_sem.at[j]).wait_send()
        whole(first, last, send_c, got_c, sc_sem.at[j], rc_sem.at[j]).wait_send()
    every_t.wait_send()
    every_d = whole(1, n, send_d, got_d, sd_sem, rd_sem)
    every_d.wait_send()
    every_d.wait_recv()


def store_kernel(got_d, back, d_prob, wg, dtok_hbm, dprob_hbm, wg_hbm, d_tokens, sem):
    cut = wg.shape[2] // 2
    stores = [
        pltpu.make_async_copy(
            wg.at[0, j, pl.ds(h * cut, cut)], wg_hbm.at[0, j, pl.ds(h * cut, cut)],
            sem.at[2 * j + h],
        )
        for j in range(3)
        for h in range(2)
    ]
    stores.append(pltpu.make_async_copy(d_prob, dprob_hbm, sem.at[6]))
    last = pltpu.make_async_copy(d_tokens, dtok_hbm, sem.at[7])
    for store in stores:
        store.start()
    rows = d_tokens.shape[0]
    pw = got_d.shape[1]
    parts = d_tokens.shape[1] // pw
    for p in range(parts):
        picked = dot(back[p * rows:(p + 1) * rows, :], got_d[...])
        d_tokens[:, p * pw:(p + 1) * pw] = picked.astype(BF16)
    last.start()
    for store in stores:
        store.wait()
    last.wait()


def shards(n, tokens, grad_out, route_prob, block_expert, block_live, expert_weights):
    rows, width = tokens.shape
    blk = rows // block_expert.shape[0]
    ff = expert_weights.shape[3]
    parts = SLOT // blk
    pw = width // parts
    group = min(n // 4, 4)
    lanes = min(rows, 128)
    slots = (n * SLOT, pw)
    every = n * blk
    vmem = pl.BlockSpec(memory_space=pltpu.VMEM)
    any_ = pl.BlockSpec(memory_space=pl.ANY)
    dma = pltpu.SemaphoreType.DMA
    shapes = (
        ((rows, width), BF16),
        ((rows // lanes, lanes), F32),
        ((1, 3, width, ff), BF16),
    )
    results = pl.pallas_call(
        functools.partial(kernel, n, blk, group),
        out_shape=(
            pltpu.VMEM(slots, BF16),
            pltpu.VMEM((parts * rows, n * SLOT), BF16),
            *[pltpu.VMEM(*shape) for shape in shapes[1:]],
        ),
        in_specs=[any_] * 6,
        out_specs=(vmem,) * 4,
        scratch_shapes=[
            pltpu.VMEM((rows, width), BF16),
            pltpu.VMEM((rows, width), BF16),
            pltpu.VMEM((rows // lanes, lanes), F32),
            pltpu.SMEM(block_expert.shape, jnp.int32),
            pltpu.SMEM(block_live.shape, jnp.int32),
            pltpu.VMEM((width, 2 * ff), BF16),
            pltpu.VMEM((2 * ff, width), BF16),
            pltpu.VMEM((width, ff), BF16),
            *[pltpu.VMEM(slots, BF16) for _ in range(5)],
            *[pltpu.VMEM((n, 1, 128), F32) for _ in range(2)],
            pltpu.VMEM((every, width), BF16),
            pltpu.VMEM((every, width), BF16),
            pltpu.VMEM((every, 2 * ff), F32),
            pltpu.VMEM((every, ff), BF16),
            dma((5,)),
            dma((3,)),
            *[dma((2,)) for _ in range(4)],
            *[dma for _ in range(4)],
        ],
        compiler_params=pltpu.CompilerParams(
            collective_id=0, has_side_effects=True, vmem_limit_bytes=40 * 1024 * 1024
        ),
        cost_estimate=pl.CostEstimate(
            flops=2 * every * width * ff * 8,
            bytes_accessed=2 * 3 * width * ff * 2,
            transcendentals=every * ff,
        ),
    )(
        *[
            pltpu.with_memory_space_constraint(value, pltpu.HBM)
            for value in (
                tokens, grad_out, route_prob.reshape(rows // lanes, lanes),
                block_expert, block_live, expert_weights,
            )
        ]
    )
    d_tokens, d_prob, weight_grads = pl.pallas_call(
        store_kernel,
        out_shape=tuple(jax.ShapeDtypeStruct(*shape) for shape in shapes),
        in_specs=[vmem] * 4,
        out_specs=(any_,) * 3,
        scratch_shapes=[pltpu.VMEM((rows, width), BF16), dma((8,))],
        compiler_params=pltpu.CompilerParams(vmem_limit_bytes=8 * 1024 * 1024),
    )(*results)
    return (d_tokens, d_prob.reshape(rows), weight_grads)


def solution(mesh):
    placed = (
        P(("groups", "expert"), None),
        P(("groups", "expert"), None),
        P(("groups", "expert")),
        P(("groups", "expert")),
        P(("groups", "expert")),
        P("expert", None, None, None),
    )
    return jax.shard_map(
        functools.partial(shards, mesh.shape["expert"]),
        mesh=mesh,
        in_specs=placed,
        out_specs=(
            P(("groups", "expert"), None),
            P(("groups", "expert")),
            P(("groups", "expert"), None, None, None),
        ),
        check_vma=False,
    )
```
